128 devices in a mesh: row: 32 (over x, y, core), col: 4 (over z).
Axes of the slice: x: 4, y: 4, z: 4, core: 2. Of those that a mesh axis runs over, the one named last changes fastest.
Arguments:
- factor_blocks: bfloat16 [512, 20, 128, 128], P('row', 'col'), may hold values from -0.125 to 0.125
- pattern: int32 [512, 20], P('row', 'col'), may hold values from -1 to 511, as said below
- levels: int32 [512], replicated, may hold values from 0 to 7, as said below
- diag_inverse: float32 [512, 128, 128], P('row')
- right_side: float32 [512, 128, 128], P('row', None, 'col'), may hold values from -6 to 6
Outputs:
- solution: float32 [512, 128, 128], P('row', None, 'col')
The draws below stay inside these ranges and needn't reach their ends.
Inputs may be any that keep to these rules, and one draw needn't show every extreme that they name: `levels`: each index of row holds 16 consecutive block rows in nondecreasing level order, 1 to 3 of them at every level, 3 at some level. `pattern`: block rows at level 0 have only empty slots; others have between 10 and 20 nonempty slots first, each naming a block row of a lower level.
All inputs are finite; a program needn't handle non-finite values.
Results may differ from the reference program's by a relative error of at most 0.0027.
Values may be sent and summed in bfloat16 or wider, within the bound.
A program may use at most 128 MiB of HBM per device.

```python
import jax
import jax.numpy as jnp
from jax import lax

B = 128
K = 20
LEV = 8
RHS = 128
BR_DEV = 16
NB = 512


def level_table(key):
    row_groups = NB // BR_DEV

    def single(sub_key):
        key_one, key_two = jax.random.split(sub_key)
        plus_count = jax.random.randint(key_one, (), 1, LEV // 2 + 1)
        ranking = jnp.argsort(jax.random.permutation(key_two, LEV)).astype(jnp.int32)
        counts = 2 + (ranking < plus_count).astype(jnp.int32) - (ranking >= LEV - plus_count).astype(jnp.int32)
        return jnp.repeat(jnp.arange(LEV, dtype=jnp.int32), counts, total_repeat_length=BR_DEV)
    keys = jax.random.split(jax.random.fold_in(key, 11), row_groups)
    return jax.vmap(single)(keys).reshape(NB).astype(jnp.int32)


def draw_levels(key, part):
    return level_table(key)


def draw_pattern(key, part):
    level_all = level_table(key)
    histogram = jnp.sum((level_all[:, None] == jnp.arange(LEV, dtype=jnp.int32)[None, :]).astype(jnp.int32), axis=0)
    before = jnp.cumsum(histogram) - histogram
    below = before[level_all]
    order = jnp.argsort(level_all, stable=True).astype(jnp.int32)
    key_one, key_two = jax.random.split(jax.random.fold_in(key, 23))
    picks = jax.random.randint(key_one, (NB, K), 0, jnp.maximum(below, 1)[:, None])
    columns = order[picks]
    real_count = jax.random.randint(key_two, (NB, 1), K // 2, K + 1)
    keep = (jnp.arange(K)[None, :] < real_count) & (level_all[:, None] > 0)
    return jnp.where(keep, columns, -1).astype(jnp.int32)


def draw_diag_inverse(key, part):
    key_one, key_two = jax.random.split(jax.random.fold_in(key, 37))
    diagonal = jax.random.uniform(key_one, (NB, B), jnp.float32, 0.7, 1.3)
    spread = jax.random.normal(key_two, (NB, B, B), jnp.float32) * (0.3 / B ** 0.5)
    strict = jnp.tril(jnp.ones((B, B), jnp.float32), -1)
    return spread * strict[None] + jnp.eye(B, dtype=jnp.float32)[None] * diagonal[:, :, None]


def block_scale(own_key, shape, cuts, low, high):
    level = 1.0
    for position, shards_of in cuts:
        heights = jax.random.uniform(jax.random.fold_in(jax.random.fold_in(own_key, 6), position), (shards_of,), jnp.float32, low / len(cuts), high / len(cuts))
        level = level * jnp.repeat(jnp.exp(heights), shape[position] // shards_of).reshape((-1,) + (1,) * (len(shape) - 1 - position))
    return level


def normal_values(key, extent, deviation, limit, cuts=(), kind=jnp.bfloat16):
    level = block_scale(key, extent, cuts, -0.22, 0.18) if cuts else 1.0
    array = jax.random.normal(key, extent, jnp.float32) * deviation * level
    return jnp.minimum(jnp.maximum(array, -limit), limit).astype(kind)


def setup_inputs(seed: int = 0) -> dict:
    key_list = jax.random.split(jax.random.key(seed), 6)
    factor_blocks = normal_values(key_list[0], (NB, K, B, B), (K * B) ** -0.5, 0.125, ((0, 32), (1, 4)))
    pattern = draw_pattern(jax.random.fold_in(key_list[5], 71), 0)
    levels = draw_levels(jax.random.fold_in(key_list[5], 71), 0)
    diag_inverse = draw_diag_inverse(jax.random.fold_in(key_list[5], 71), 0)
    right_side = normal_values(key_list[4], (NB, B, RHS), 1.0, 6.0, ((0, 32), (2, 4)), jnp.float32)
    return {"factor_blocks": factor_blocks, "pattern": pattern, "levels": levels, "diag_inverse": diag_inverse, "right_side": right_side}


def reference(factor_blocks, pattern, levels, diag_inverse, right_side):
    order = jnp.argsort(levels, stable=True).astype(jnp.int32)
    solved_table = jnp.zeros(right_side.shape, jnp.bfloat16)
    solution = jnp.zeros(right_side.shape, jnp.float32)

    def advance(carry, g_index):
        solved_table, solution = carry
        columns = pattern[g_index]
        present = columns >= 0
        lookup = jnp.where(present, columns, 0).astype(jnp.int32)
        pieces = solved_table[lookup].astype(jnp.float32) * present[:, None, None].astype(jnp.float32)
        partial_sum = jnp.einsum('kab,kbr->ar', factor_blocks[g_index].astype(jnp.float32), pieces)
        solved = jnp.dot(diag_inverse[g_index], right_side[g_index] - partial_sum, precision=lax.Precision.HIGHEST)
        solved_table = solved_table.at[g_index].set(solved.astype(jnp.bfloat16))
        solution = solution.at[g_index].set(solved)
        return (solved_table, solution), None

    (solved_table, solution), _ = lax.scan(advance, (solved_table, solution), order)
    return solution
```

```python
import jax
import jax.numpy as jnp
from jax import lax
from jax.experimental import pallas as pl
from jax.experimental.pallas import tpu as pltpu
from jax.sharding import PartitionSpec as P

MESH = pl.DeviceIdType.MESH
LEV = 8
CAP = 3
B = 128
W = 16
ROWS = 16
SLOTS = 5
EMPTY = (LEV - 1) * CAP * 32
ORDERS = ((0, 1, 2), (1, 2, 0), (2, 0, 1))


def dot_t(a, b):
    return lax.dot_general(a, b, (((1,), (1,)), ((), ())), preferred_element_type=jnp.float32)


def split(a):
    high = a.astype(jnp.bfloat16)
    return high, (a - high.astype(jnp.float32)).astype(jnp.bfloat16)


def times_inverse(v, d):
    n = v.shape[0]
    v_high, v_low = split(v)
    d_high, d_low = split(d)
    both = dot_t(jnp.concatenate([v_high, v_low], axis=0), d_high)
    return both[:n] + (both[n:] + dot_t(v_high, d_low))


def kernel(
    factor, pattern, levels, inverse, rhs, out,
    blocks, inv0, inv, rhs_other, pat_other, table, land, sums, sums_in, x0, x0_in, sol, sol_other, lookup, rows,
    local_sem, start_s, start_r, p0s, p0r, p1s, p1r, p2s, p2r, red_s, red_r, sol_s, sol_r,
):
    row, z = lax.axis_index("row"), lax.axis_index("col")
    x, y, q = row // 8, lax.rem(row // 2, 4), lax.rem(row, 2)
    me = (x, y, z)
    other = 1 - q

    def device(xyz, core):
        return ((xyz[0] * 4 + xyz[1]) * 2 + core, xyz[2])

    def moved(dim, by):
        xyz = list(me)
        xyz[dim] = lax.rem(me[dim] + by, 4)
        return device(xyz, q)

    partner = device(me, other)

    def remote(src, dst, s, r, to):
        return pltpu.make_async_remote_copy(
            src_ref=src, dst_ref=dst, send_sem=s, recv_sem=r, device_id=to, device_id_type=MESH
        )

    own = [
        pltpu.make_async_copy(inverse.at[0:CAP], inv0, local_sem.at[0]),
        pltpu.make_async_copy(inverse, inv.at[0], local_sem.at[1]),
        pltpu.make_async_copy(factor, blocks.at[0], local_sem.at[2]),
    ]
    for c in own:
        c.start()

    barrier = pltpu.get_barrier_semaphore()
    greeted = [partner] + [moved(d, by) for d in range(3) for by in (1, 2, 3)]
    for to in greeted:
        pl.semaphore_signal(barrier, inc=1, device_id=to, device_id_type=MESH)
    table[EMPTY] = jnp.zeros(table.shape[1:], table.dtype)
    pl.semaphore_wait(barrier, len(greeted))

    def start_copies():
        return [
            remote(pattern, pat_other, start_s.at[0], start_r.at[0], partner),
            remote(rhs.at[:, other], rhs_other, start_s.at[1], start_r.at[1], partner),
            remote(inverse, inv.at[1], start_s.at[2], start_r.at[2], partner),
            remote(factor, blocks.at[1], start_s.at[3], start_r.at[3], partner),
        ]

    x0_copy = remote(x0.at[other], x0_in, start_s.at[4], start_r.at[4], partner)

    def place(c):
        d0, d1, d2 = ORDERS[c]
        return me[d2] * 16 + me[d1] * 4 + me[d0]

    own[0].wait()
    for c in range(CAP):
        v = times_inverse(rhs[c].reshape(2 * W, B), inv0[c]).reshape(2, W, B)
        sol[:, c] = v
        x0[:, c] = v.astype(jnp.bfloat16)
    x0_copy.start()
    for copy in start_copies():
        copy.start()
    for c in range(CAP):
        land[0, c, place(c), q] = x0[q, c]
    x0_copy.wait()
    for c in range(CAP):
        land[0, c, place(c), other] = x0_in[c]

    def phase0(p, c):
        d0 = ORDERS[c][0]
        unit = land.at[p, c, pl.ds(place(c), 1)]
        return [
            remote(unit, unit, p0s.at[p, 3 * c + by - 1], p0r.at[p, 3 * c + by - 1], moved(d0, by)) for by in (1, 2, 3)
        ]

    def phase0_in(p, c):
        d0, d1, d2 = ORDERS[c]
        result = []
        for by in (1, 2, 3):
            at = me[d2] * 16 + me[d1] * 4 + lax.rem(me[d0] + 4 - by, 4)
            unit = land.at[p, c, pl.ds(at, 1)]
            result.append(remote(unit, unit, p0s.at[p, 3 * c + by - 1], p0r.at[p, 3 * c + by - 1], moved(d0, by)))
        return result

    def phase1(p, c):
        d0, d1, d2 = ORDERS[c]
        unit = land.at[p, c, pl.ds(me[d2] * 16 + me[d1] * 4, 4)]
        return [
            remote(unit, unit, p1s.at[p, 3 * c + by - 1], p1r.at[p, 3 * c + by - 1], moved(d1, by)) for by in (1, 2, 3)
        ]

    def phase1_in(p, c):
        d0, d1, d2 = ORDERS[c]
        result = []
        for by in (1, 2, 3):
            unit = land.at[p, c, pl.ds(me[d2] * 16 + lax.rem(me[d1] + 4 - by, 4) * 4, 4)]
            result.append(remote(unit, unit, p1s.at[p, 3 * c + by - 1], p1r.at[p, 3 * c + by - 1], moved(d1, by)))
        return result

    RING = ((0, 0, 1), (0, 1, 1), (0, 1, 3), (0, 0, 3), (3, 0, 1), (1, 1, 3))

    def phase2(p, c, k):
        d2 = ORDERS[c][2]
        owner, half, to = RING[k]
        unit = land.at[p, c, pl.ds(lax.rem(me[d2] + owner, 4) * 16 + half * 8, 8)]
        return remote(unit, unit, p2s.at[p, 6 * c + k], p2r.at[p, 6 * c + k], moved(d2, to))

    def phase2_in(p, c, k):
        d2 = ORDERS[c][2]
        owner, half, to = RING[k]
        unit = land.at[p, c, pl.ds(lax.rem(me[d2] + owner + 4 - to, 4) * 16 + half * 8, 8)]
        return remote(unit, unit, p2s.at[p, 6 * c + k], p2r.at[p, 6 * c + k], moved(d2, to))

    def sums_copy(p, by):
        to = lax.rem(z + by, 4)
        return remote(sums.at[to], sums_in.at[by - 1], red_s.at[p, by - 1], red_r.at[p, by - 1], moved(2, by))

    def sol_copy(level):
        at = pl.ds(level * CAP, CAP)
        return remote(sol_other.at[at], sol.at[q, at], sol_s.at[level], sol_r.at[level], partner)

    for c in range(CAP):
        for copy in phase0(0, c):
            copy.start()

    def find(level):
        for s in range(2):
            first = (row + s - 2 * s * q) * ROWS
            start = jnp.int32(0)
            for r in range(ROWS):
                start += (levels[first + r] < level).astype(jnp.int32)
            for c in range(CAP):
                r = jnp.minimum(start + c, ROWS - 1)
                rows[s * CAP + c] = r
                for k in range(SLOTS):
                    j = pattern[r, k] if s == 0 else pat_other[r, k]
                    j0 = jnp.maximum(j, 0)
                    inside = lax.rem(j0, ROWS)
                    its = levels[j0]
                    rank = ((levels[jnp.maximum(j0 - 1, 0)] == its) & (inside >= 1)).astype(jnp.int32) + (
                        (levels[jnp.maximum(j0 - 2, 0)] == its) & (inside >= 2)
                    ).astype(jnp.int32)
                    slot = (its * CAP + rank) * 32 + j0 // ROWS
                    slot = jnp.where(j < 0, EMPTY, jnp.minimum(slot, EMPTY))
                    lookup[(s * CAP + c) * SLOTS + k] = slot

    def body(level, carry):
        p = lax.rem(level - 1, 2)
        p_next = lax.rem(level, 2)
        for c in range(CAP):
            for copy in phase0_in(p, c):
                copy.wait_recv()
            for copy in phase1(p, c):
                copy.start()
        for c in range(CAP):
            for copy in phase1_in(p, c):
                copy.wait_recv()
            for k in (0, 2, 1, 3):
                phase2(p, c, k).start()

        @pl.when(level == 1)
        def _():
            for copy in start_copies():
                copy.wait()
            own[1].wait()
            own[2].wait()

        find(level)
        for c in range(CAP):
            phase2_in(p, c, 0).wait_recv()
            phase2(p, c, 4).start()
            phase2_in(p, c, 2).wait_recv()
            phase2(p, c, 5).start()
        for c in range(CAP):
            for k in (1, 3, 4, 5):
                phase2_in(p, c, k).wait_recv()
        for c in range(CAP):
            for copy in phase0(p, c) + phase1(p, c) + [phase2(p, c, k) for k in range(6)]:
                copy.wait_send()

        def to_table(i, carry):
            a, b = i // 4, lax.rem(i, 4)
            for c in range(CAP):
                at = ((level - 1) * CAP + c) * 32 + i * 2
                for e in range(4):
                    xyz = (a, b, e)
                    d0, d1, d2 = ORDERS[c]
                    from_ = xyz[d2] * 16 + xyz[d1] * 4 + xyz[d0]
                    for core in range(2):
                        table[at + core, e] = land[p, c, from_, core]
            return carry

        lax.fori_loop(0, 16, to_table, 0)

        for s in range(2):
            for c in range(CAP):
                i = s * CAP + c
                r = rows[i]
                total = None
                for k in range(SLOTS):
                    piece = table[lookup[i * SLOTS + k]].reshape(4 * W, B)
                    term = dot_t(piece, blocks[s, r, k])
                    total = term if total is None else total + term
                sums[:, i] = total.reshape(4, W, B)
        for by in (2, 1, 3):
            sums_copy(p, by).start()
        for by in (2, 1, 3):
            sums_copy(p, by).wait()

        for s in range(2):
            for c in range(CAP):
                i = s * CAP + c
                r = rows[i]
                total = (sums[z, i] + sums_in[0, i]) + (sums_in[1, i] + sums_in[2, i])
                mine = rhs[r, q] if s == 0 else rhs_other[r]
                v = times_inverse(mine - total, inv[s, r])
                if s == 0:
                    sol[q, level * CAP + c] = v
                    land[p_next, c, place(c), q] = v.astype(jnp.bfloat16)
                else:
                    sol_other[level * CAP + c] = v
                    land[p_next, c, place(c), other] = v.astype(jnp.bfloat16)

        @pl.when(level < LEV - 1)
        def _():
            for c in range(CAP):
                for copy in phase0(p_next, c):
                    copy.start()

        sol_copy(level).start()
        return carry

    lax.fori_loop(1, LEV, body, 0)

    for level in range(1, LEV):
        sol_copy(level).wait_send()
    for level in range(1, LEV):
        at = pl.ds(level * CAP, CAP)
        remote(sol_other.at[at], sol.at[other, at], sol_s.at[level], sol_r.at[level], partner).wait_recv()
    for r in range(ROWS):
        its = levels[row * ROWS + r]
        rank = jnp.int32(0)
        for back in (1, 2):
            if r >= back:
                rank += (levels[row * ROWS + r - back] == its).astype(jnp.int32)
        at = its * CAP + rank
        out[r, 0] = sol[0, at]
        out[r, 1] = sol[1, at]


def per_device(factor_blocks, pattern, levels, diag_inverse, right_side):
    rhs = jnp.swapaxes(right_side, 1, 2).reshape(ROWS, 2, W, B)
    bf, f32, dma = jnp.bfloat16, jnp.float32, pltpu.SemaphoreType.DMA
    vmem = pltpu.VMEM
    out = pl.pallas_call(
        kernel,
        out_shape=jax.ShapeDtypeStruct((ROWS, 2, W, B), f32),
        in_specs=[
            pl.BlockSpec(memory_space=pl.ANY),
            pl.BlockSpec(memory_space=pltpu.SMEM),
            pl.BlockSpec(memory_space=pltpu.SMEM),
            pl.BlockSpec(memory_space=pl.ANY),
            pl.BlockSpec(memory_space=pltpu.VMEM),
        ],
        out_specs=pl.BlockSpec(memory_space=pltpu.VMEM),
        scratch_shapes=[
            vmem((2, ROWS, SLOTS, B, B), bf),
            vmem((CAP, B, B), f32),
            vmem((2, ROWS, B, B), f32),
            vmem((ROWS, W, B), f32),
            pltpu.SMEM((ROWS, SLOTS), jnp.int32),
            vmem((EMPTY + 1, 4, W, B), bf),
            vmem((2, CAP, 64, 2, W, B), bf),
            vmem((4, 2 * CAP, W, B), f32),
            vmem((3, 2 * CAP, W, B), f32),
            vmem((2, CAP, W, B), bf),
            vmem((CAP, W, B), bf),
            vmem((2, LEV * CAP, W, B), f32),
            vmem((LEV * CAP, W, B), f32),
            pltpu.SMEM((2 * CAP * SLOTS,), jnp.int32),
            pltpu.SMEM((2 * CAP,), jnp.int32),
            dma((3,)), dma((5,)), dma((5,)),
            dma((2, 9)), dma((2, 9)), dma((2, 9)), dma((2, 9)), dma((2, 18)), dma((2, 18)),
            dma((2, 3)), dma((2, 3)), dma((LEV,)), dma((LEV,)),
        ],
        compiler_params=pltpu.CompilerParams(
            collective_id=0, has_side_effects=True, vmem_limit_bytes=48 * 1024 * 1024
        ),
    )(factor_blocks, pattern, levels, diag_inverse, rhs)
    return jnp.swapaxes(out.reshape(ROWS, 2 * W, B), 1, 2)


def solution(mesh):
    return jax.shard_map(
        per_device,
        mesh=mesh,
        in_specs=(
            P("row", "col", None, None),
            P("row", "col"),
            P(),
            P("row", None, None),
            P("row", None, "col"),
        ),
        out_specs=P("row", None, "col"),
        check_vma=False,
    )
```

```python
import jax
import jax.numpy as jnp
from jax import lax
from jax.experimental import pallas as pl
from jax.experimental.pallas import tpu as pltpu
from jax.sharding import PartitionSpec as P

MESH = pl.DeviceIdType.MESH
LEV = 8
CAP = 3
B = 128
W = 32
ROWS = 16
SLOTS = 5
EMPTY = (LEV - 1) * 32 * CAP
EARLY = 6
AHEAD = 3


def dot_t(a, b):
    return lax.dot_general(a, b, (((1,), (1,)), ((), ())), preferred_element_type=jnp.float32)


def split(a):
    high = a.astype(jnp.bfloat16)
    return high, (a - high.astype(jnp.float32)).astype(jnp.bfloat16)


def times_inverse(v, d):
    n = v.shape[0]
    v_high, v_low = split(v)
    d_high, d_low = split(d)
    both = dot_t(jnp.concatenate([v_high, v_low], axis=0), d_high)
    return both[:n] + (both[n:] + dot_t(v_high, d_low))


def kernel(
    factor, pattern, levels, inverse, rhs, out,
    blocks, late, inv0, inv, pats, table, land, sol, lookup, rows,
    local_sem, late_sem, pat_s, pat_r, zs, zr, gs, gr, cs, cr,
):
    row, z = lax.axis_index("row"), lax.axis_index("col")
    x, y, q = row // 8, lax.rem(row // 2, 4), lax.rem(row, 2)
    chip = x * 4 + y
    partner = (chip * 2 + 1 - q, z)

    def along_z(by):
        return (row, lax.rem(z + by, 4))

    def remote(src, dst, s, r, to):
        return pltpu.make_async_remote_copy(
            src_ref=src, dst_ref=dst, send_sem=s, recv_sem=r, device_id=to, device_id_type=MESH
        )

    own = [
        pltpu.make_async_copy(inverse.at[0:CAP], inv0, local_sem.at[0]),
        pltpu.make_async_copy(inverse, inv, local_sem.at[1]),
        pltpu.make_async_copy(factor.at[0:EARLY], blocks.at[0:EARLY, z], local_sem.at[2]),
        pltpu.make_async_copy(factor.at[EARLY:ROWS], late.at[:, z], local_sem.at[3]),
    ]
    for c in own:
        c.start()

    offsets = [(dx, dy) for dx in range(4) for dy in range(4) if (dx, dy) != (0, 0)]
    offsets.sort(key=lambda o: -(min(o[0], 4 - o[0]) + min(o[1], 4 - o[1])))

    def in_plane(dx, dy):
        return ((lax.rem(x + dx, 4) * 4 + lax.rem(y + dy, 4)) * 2 + q, z)

    barrier = pltpu.get_barrier_semaphore()
    greeted = [partner] + [along_z(by) for by in (1, 2, 3)] + [in_plane(*o) for o in offsets]
    for to in greeted:
        pl.semaphore_signal(barrier, inc=1, device_id=to, device_id_type=MESH)
    table[EMPTY] = jnp.zeros(table.shape[1:], table.dtype)
    pl.semaphore_wait(barrier, len(greeted))

    def home(t, owner):
        if isinstance(t, int) and t < EARLY:
            return blocks.at[t, owner]
        return late.at[t - EARLY, owner]

    def direct(t):
        return [remote(factor.at[t], home(t, z), zs.at[t, k], zr.at[t, k], along_z(1 + 2 * k)) for k in range(2)]

    def arrives(t, k, owner):
        unit = home(t, owner)
        return remote(unit, unit, zs.at[t, k], zr.at[t, k], along_z(1))

    def forward(t):
        by = 1 + 2 * lax.rem(t + q, 2)
        unit = home(t, lax.rem(z + 4 - by, 4))
        return remote(unit, unit, zs.at[t, 2], zr.at[t, 2], along_z(by))

    def pass_on(t):
        k = lax.rem(t + q, 2)
        arrives(t, k, lax.rem(z + 3 - 2 * k, 4)).wait_recv()
        forward(t).start()

    def send_ahead(t):
        for copy in direct(t):
            copy.start()

    def arrive(t):
        k = lax.rem(t + q, 2)
        arrives(t, 1 - k, lax.rem(z + 1 + 2 * k, 4)).wait_recv()
        arrives(t, 2, lax.rem(z + 2, 4)).wait_recv()

    for t in range(1, 1 + AHEAD):
        send_ahead(t)

    def pattern_copies():
        return [remote(pattern, pats.at[3 - by], pat_s.at[by - 1], pat_r.at[by - 1], along_z(by)) for by in (1, 2, 3)]

    def pattern_arrives():
        return [remote(pats.at[3 - by], pats.at[3 - by], pat_s.at[by - 1], pat_r.at[by - 1], along_z(by)) for by in (1, 2, 3)]

    def spread(p, dx, dy):
        unit = land.at[p, q, x, y]
        return remote(unit, unit, gs.at[p, dx, dy], gr.at[p, dx, dy], in_plane(dx, dy))

    def spread_in(p, dx, dy):
        unit = land.at[p, q, lax.rem(x + 4 - dx, 4), lax.rem(y + 4 - dy, 4)]
        return remote(unit, unit, gs.at[p, dx, dy], gr.at[p, dx, dy], in_plane(dx, dy))

    def across(p, dx, core):
        unit = land.at[p, core, lax.rem(x + 4 - dx, 4)]
        return remote(unit, unit, cs.at[p, dx], cr.at[p, dx], partner)

    def start_spread(p):
        for o in offsets:
            spread(p, *o).start()

    own[0].wait()
    for c in range(CAP):
        v = times_inverse(rhs[c], inv0[c])
        sol[c] = v
        land[0, q, x, y, c] = v.astype(jnp.bfloat16)
    start_spread(0)
    for copy in pattern_copies():
        copy.start()

    def find(level):
        first = row * ROWS
        start = jnp.int32(0)
        for r in range(ROWS):
            start += (levels[first + r] < level).astype(jnp.int32)
        for c in range(CAP):
            r = jnp.minimum(start + c, ROWS - 1)
            rows[c] = r
            for k in range(4 * SLOTS):
                far, slot = k // SLOTS, k % SLOTS
                j = pattern[r, slot] if far == 0 else pats[far - 1, r, slot]
                j0 = jnp.maximum(j, 0)
                inside = lax.rem(j0, ROWS)
                its = levels[j0]
                rank = ((levels[jnp.maximum(j0 - 1, 0)] == its) & (inside >= 1)).astype(jnp.int32) + (
                    (levels[jnp.maximum(j0 - 2, 0)] == its) & (inside >= 2)
                ).astype(jnp.int32)
                group = j0 // ROWS
                at = ((its * 2 + lax.rem(group, 2)) * 16 + group // 2) * CAP + rank
                lookup[c * 4 * SLOTS + k] = jnp.where(j < 0, EMPTY, jnp.minimum(at, EMPTY))

    def from_late(t):
        return pltpu.make_async_copy(late.at[t - EARLY], blocks.at[t], late_sem.at[t - EARLY])

    def body(level, carry):
        p = lax.rem(level - 1, 2)
        p_next = lax.rem(level, 2)

        @pl.when(level == 1)
        def _():
            pass_on(1)
            send_ahead(1 + AHEAD)

        @pl.when((level >= 2) & (level <= 4))
        def _():
            pass_on(3 * level)
            send_ahead_late(3 * level + AHEAD)

        for dx in (0, 1, 3, 2):
            for dy in (1, 3, 2, 0):
                if (dx, dy) != (0, 0):
                    spread_in(p, dx, dy).wait_recv()
            across(p, dx, q).start()

        @pl.when(level == 1)
        def _():
            for copy in pattern_arrives():
                copy.wait_recv()
            for copy in pattern_copies():
                copy.wait_send()

        find(level)

        @pl.when(level == 1)
        def _():
            for t in range(2, EARLY):
                pass_on(t)
                send_ahead(t + AHEAD)
            for t in range(1, EARLY):
                arrive(t)
            for copy in own[1:]:
                copy.wait()

        @pl.when((level >= 2) & (level <= 4))
        def _():
            for i in (1, 2):
                pass_on(3 * level + i)
                send_ahead_late(3 * level + i + AHEAD)
            for i in range(3):
                arrive(3 * level + i)
                from_late(3 * level + i).start()

        @pl.when(level == 5)
        def _():
            pass_on(jnp.int32(15))
            arrive(jnp.int32(15))
            from_late(jnp.int32(15)).start()

        for o in offsets:
            spread(p, *o).wait_send()
        for dx in range(4):
            across(p, dx, q).wait_send()
            across(p, dx, 1 - q).wait_recv()

        def to_table(i, carry):
            a, b = i // 4, lax.rem(i, 4)
            for core in range(2):
                for c in range(CAP):
                    table[(((level - 1) * 2 + core) * 16 + i) * CAP + c] = land[p, core, a, b, c]
            return carry

        lax.fori_loop(0, 16, to_table, 0)

        @pl.when((level >= 2) & (level <= 4))
        def _():
            for i in range(3):
                from_late(3 * level + i).wait()

        @pl.when(level == 5)
        def _():
            from_late(jnp.int32(15)).wait()

        for c in range(CAP):
            r = rows[c]
            total = None
            for k in range(0, 4 * SLOTS, 2):
                pieces = [table[lookup[c * 4 * SLOTS + k + i]] for i in range(2)]
                factors = [blocks[r, lax.rem(z + (k + i) // SLOTS, 4), (k + i) % SLOTS] for i in range(2)]
                term = dot_t(jnp.concatenate(pieces, axis=1), jnp.concatenate(factors, axis=1))
                total = term if total is None else total + term
            v = times_inverse(rhs[r] - total, inv[r])
            sol[level * CAP + c] = v
            land[p_next, q, x, y, c] = v.astype(jnp.bfloat16)

        @pl.when(level < LEV - 1)
        def _():
            start_spread(p_next)

        return carry

    def send_ahead_late(t):
        @pl.when(t <= ROWS - 1)
        def _():
            send_ahead(t)

    lax.fori_loop(1, LEV, body, 0)

    for t in range(1, ROWS):
        for copy in direct(t) + [forward(t)]:
            copy.wait_send()
    for r in range(ROWS):
        its = levels[row * ROWS + r]
        rank = jnp.int32(0)
        for back in (1, 2):
            if r >= back:
                rank += (levels[row * ROWS + r - back] == its).astype(jnp.int32)
        out[r] = sol[its * CAP + rank]


def per_device(factor_blocks, pattern, levels, diag_inverse, right_side):
    rhs = jnp.swapaxes(right_side, 1, 2)
    bf, f32, dma = jnp.bfloat16, jnp.float32, pltpu.SemaphoreType.DMA
    vmem = pltpu.VMEM
    out = pl.pallas_call(
        kernel,
        out_shape=jax.ShapeDtypeStruct((ROWS, W, B), f32),
        in_specs=[
            pl.BlockSpec(memory_space=pl.ANY),
            pl.BlockSpec(memory_space=pltpu.SMEM),
            pl.BlockSpec(memory_space=pltpu.SMEM),
            pl.BlockSpec(memory_space=pl.ANY),
            pl.BlockSpec(memory_space=pltpu.VMEM),
        ],
        out_specs=pl.BlockSpec(memory_space=pltpu.VMEM),
        scratch_shapes=[
            vmem((ROWS, 4, SLOTS, B, B), bf),
            vmem((ROWS - EARLY, 4, SLOTS, B, B), bf),
            vmem((CAP, B, B), f32),
            vmem((ROWS, B, B), f32),
            pltpu.SMEM((3, ROWS, SLOTS), jnp.int32),
            vmem((EMPTY + 1, W, B), bf),
            vmem((2, 2, 4, 4, CAP, W, B), bf),
            vmem((LEV * CAP, W, B), f32),
            pltpu.SMEM((CAP * 4 * SLOTS,), jnp.int32),
            pltpu.SMEM((CAP,), jnp.int32),
            dma((4,)), dma((ROWS - EARLY,)), dma((3,)), dma((3,)),
            dma((ROWS, 3)), dma((ROWS, 3)),
            dma((2, 4, 4)), dma((2, 4, 4)), dma((2, 4)), dma((2, 4)),
        ],
        compiler_params=pltpu.CompilerParams(
            collective_id=0, has_side_effects=True, vmem_limit_bytes=56 * 1024 * 1024
        ),
    )(factor_blocks, pattern, levels, diag_inverse, rhs)
    return jnp.swapaxes(out, 1, 2)


def solution(mesh):
    return jax.shard_map(
        per_device,
        mesh=mesh,
        in_specs=(
            P("row", "col", None, None),
            P("row", "col"),
            P(),
            P("row", None, None),
            P("row", None, "col"),
        ),
        out_specs=P("row", None, "col"),
        check_vma=False,
    )
```

```python
import jax
import jax.numpy as jnp
from jax import lax
from jax.experimental import pallas as pl
from jax.experimental.pallas import tpu as pltpu
from jax.sharding import PartitionSpec as P

MESH = pl.DeviceIdType.MESH
LEV = 8
CAP = 3
B = 128
W = 32
ROWS = 16
SLOTS = 5
EMPTY = (LEV - 1) * 32 * CAP
EARLY = 6
AHEAD = 3


def dot_t(a, b):
    return lax.dot_general(a, b, (((1,), (1,)), ((), ())), preferred_element_type=jnp.float32)


def split(a):
    high = a.astype(jnp.bfloat16)
    return high, (a - high.astype(jnp.float32)).astype(jnp.bfloat16)


def times_inverse(v, d):
    n = v.shape[0]
    v_high, v_low = split(v)
    d_high, d_low = split(d)
    both = dot_t(jnp.concatenate([v_high, v_low], axis=0), d_high)
    return both[:n] + (both[n:] + dot_t(v_high, d_low))


def kernel(
    factor, pattern, levels, inverse, rhs, out,
    blocks, late, inv0, inv, pats, table, land, sol, lookup, rows,
    local_sem, late_sem, pat_s, pat_r, zs, zr, gs, gr, cs, cr,
):
    row, z = lax.axis_index("row"), lax.axis_index("col")
    x, y, q = row // 8, lax.rem(row // 2, 4), lax.rem(row, 2)
    chip = x * 4 + y
    partner = (chip * 2 + 1 - q, z)

    def along_z(by):
        return (row, lax.rem(z + by, 4))

    def remote(src, dst, s, r, to):
        return pltpu.make_async_remote_copy(
            src_ref=src, dst_ref=dst, send_sem=s, recv_sem=r, device_id=to, device_id_type=MESH
        )

    own = [
        pltpu.make_async_copy(inverse.at[0:CAP], inv0, local_sem.at[0]),
        pltpu.make_async_copy(inverse, inv, local_sem.at[1]),
        pltpu.make_async_copy(factor.at[0:EARLY], blocks.at[0:EARLY, z], local_sem.at[2]),
        pltpu.make_async_copy(factor.at[EARLY:ROWS], late.at[:, z], local_sem.at[3]),
    ]
    for c in own:
        c.start()

    offsets = [(dx, dy) for dx in range(4) for dy in range(4) if (dx, dy) != (0, 0)]
    offsets.sort(key=lambda o: -(min(o[0], 4 - o[0]) + min(o[1], 4 - o[1])))

    def in_plane(dx, dy):
        return ((lax.rem(x + dx, 4) * 4 + lax.rem(y + dy, 4)) * 2 + q, z)

    barrier = pltpu.get_barrier_semaphore()
    greeted = [partner] + [along_z(by) for by in (1, 2, 3)] + [in_plane(*o) for o in offsets]
    for to in greeted:
        pl.semaphore_signal(barrier, inc=1, device_id=to, device_id_type=MESH)
    table[EMPTY] = jnp.zeros(table.shape[1:], table.dtype)
    pl.semaphore_wait(barrier, len(greeted))

    def home(t, owner):
        if isinstance(t, int) and t < EARLY:
            return blocks.at[t, owner]
        return late.at[t - EARLY, owner]

    def direct(t):
        return [remote(factor.at[t], home(t, z), zs.at[t, k], zr.at[t, k], along_z(1 + 2 * k)) for k in range(2)]

    def arrives(t, k, owner):
        unit = home(t, owner)
        return remote(unit, unit, zs.at[t, k], zr.at[t, k], along_z(1))

    def forward(t):
        by = 1 + 2 * lax.rem(t + q, 2)
        unit = home(t, lax.rem(z + 4 - by, 4))
        return remote(unit, unit, zs.at[t, 2], zr.at[t, 2], along_z(by))

    def pass_on(t):
        k = lax.rem(t + q, 2)
        arrives(t, k, lax.rem(z + 3 - 2 * k, 4)).wait_recv()
        forward(t).start()

    def send_ahead(t):
        for copy in direct(t):
            copy.start()

    def arrive(t):
        k = lax.rem(t + q, 2)
        arrives(t, 1 - k, lax.rem(z + 1 + 2 * k, 4)).wait_recv()
        arrives(t, 2, lax.rem(z + 2, 4)).wait_recv()

    def pattern_copies():
        return [remote(pattern, pats.at[3 - by], pat_s.at[by - 1], pat_r.at[by - 1], along_z(by)) for by in (1, 2, 3)]

    def pattern_arrives():
        return [remote(pats.at[3 - by], pats.at[3 - by], pat_s.at[by - 1], pat_r.at[by - 1], along_z(by)) for by in (1, 2, 3)]

    for copy in pattern_copies():
        copy.start()
    for t in range(1, 1 + AHEAD):
        send_ahead(t)

    def spread(p, dx, dy):
        unit = land.at[p, q, x, y]
        return remote(unit, unit, gs.at[p, dx, dy], gr.at[p, dx, dy], in_plane(dx, dy))

    def spread_in(p, dx, dy):
        unit = land.at[p, q, lax.rem(x + 4 - dx, 4), lax.rem(y + 4 - dy, 4)]
        return remote(unit, unit, gs.at[p, dx, dy], gr.at[p, dx, dy], in_plane(dx, dy))

    def across(p, dx, core):
        unit = land.at[p, core, lax.rem(x + 4 - dx, 4)]
        return remote(unit, unit, cs.at[p, dx], cr.at[p, dx], partner)

    def start_spread(p):
        for o in offsets:
            spread(p, *o).start()

    own[0].wait()
    for c in range(CAP):
        v = times_inverse(rhs[c], inv0[c])
        sol[c] = v
        land[0, q, x, y, c] = v.astype(jnp.bfloat16)
    start_spread(0)

    def find(level):
        first = row * ROWS
        start = jnp.int32(0)
        for r in range(ROWS):
            start += (levels[first + r] < level).astype(jnp.int32)
        for c in range(CAP):
            r = jnp.minimum(start + c, ROWS - 1)
            rows[c] = r
            for k in range(4 * SLOTS):
                far, slot = k // SLOTS, k % SLOTS
                j = pattern[r, slot] if far == 0 else pats[far - 1, r, slot]
                j0 = jnp.maximum(j, 0)
                inside = lax.rem(j0, ROWS)
                its = levels[j0]
                rank = ((levels[jnp.maximum(j0 - 1, 0)] == its) & (inside >= 1)).astype(jnp.int32) + (
                    (levels[jnp.maximum(j0 - 2, 0)] == its) & (inside >= 2)
                ).astype(jnp.int32)
                group = j0 // ROWS
                at = ((its * 2 + lax.rem(group, 2)) * 16 + group // 2) * CAP + rank
                lookup[c * 4 * SLOTS + k] = jnp.where(j < 0, EMPTY, jnp.minimum(at, EMPTY))

    def from_late(t):
        return pltpu.make_async_copy(late.at[t - EARLY], blocks.at[t], late_sem.at[t - EARLY])

    def body(level, carry):
        p = lax.rem(level - 1, 2)
        p_next = lax.rem(level, 2)

        @pl.when(level == 1)
        def _():
            pass_on(1)
            send_ahead(1 + AHEAD)
            for copy in pattern_arrives():
                copy.wait_recv()
            for copy in pattern_copies():
                copy.wait_send()

        find(level)

        @pl.when((level == 2) | (level == 3))
        def _():
            pass_on(3 * level)
            send_ahead_late(3 * level + AHEAD)

        @pl.when((level == 4) | (level == 5))
        def _():
            pass_on(2 * level + 4)
            send_ahead_late(2 * level + 4 + AHEAD)

        for dx in (0, 1, 3, 2):
            for dy in (1, 3, 2, 0):
                if (dx, dy) != (0, 0):
                    spread_in(p, dx, dy).wait_recv()
            across(p, dx, q).start()

        @pl.when(level == 1)
        def _():
            for t in range(2, EARLY):
                pass_on(t)
                send_ahead(t + AHEAD)
            for t in range(1, EARLY):
                arrive(t)
            for copy in own[1:]:
                copy.wait()

        @pl.when((level == 2) | (level == 3))
        def _():
            for i in (1, 2):
                pass_on(3 * level + i)
                send_ahead_late(3 * level + i + AHEAD)
            for i in range(3):
                arrive(3 * level + i)
                from_late(3 * level + i).start()

        @pl.when((level == 4) | (level == 5))
        def _():
            pass_on(2 * level + 5)

        @pl.when(level >= 4)
        def _():
            arrive(level + 8)
            from_late(level + 8).start()

        for o in offsets:
            spread(p, *o).wait_send()
        for dx in range(4):
            across(p, dx, q).wait_send()
            across(p, dx, 1 - q).wait_recv()

        def to_table(i, carry):
            a, b = i // 4, lax.rem(i, 4)
            for core in range(2):
                for c in range(CAP):
                    table[(((level - 1) * 2 + core) * 16 + i) * CAP + c] = land[p, core, a, b, c]
            return carry

        lax.fori_loop(0, 16, to_table, 0)

        @pl.when((level == 2) | (level == 3))
        def _():
            for i in range(3):
                from_late(3 * level + i).wait()

        @pl.when(level >= 4)
        def _():
            from_late(level + 8).wait()

        for c in range(CAP):
            r = rows[c]
            total = None
            for k in range(0, 4 * SLOTS, 2):
                pieces = [table[lookup[c * 4 * SLOTS + k + i]] for i in range(2)]
                factors = [blocks[r, lax.rem(z + (k + i) // SLOTS, 4), (k + i) % SLOTS] for i in range(2)]
                term = dot_t(jnp.concatenate(pieces, axis=1), jnp.concatenate(factors, axis=1))
                total = term if total is None else total + term
            v = times_inverse(rhs[r] - total, inv[r])
            sol[level * CAP + c] = v
            land[p_next, q, x, y, c] = v.astype(jnp.bfloat16)

        @pl.when(level < LEV - 1)
        def _():
            start_spread(p_next)

        return carry

    def send_ahead_late(t):
        @pl.when(t <= ROWS - 1)
        def _():
            send_ahead(t)

    lax.fori_loop(1, LEV, body, 0)

    for t in range(1, ROWS):
        for copy in direct(t) + [forward(t)]:
            copy.wait_send()
    for r in range(ROWS):
        its = levels[row * ROWS + r]
        rank = jnp.int32(0)
        for back in (1, 2):
            if r >= back:
                rank += (levels[row * ROWS + r - back] == its).astype(jnp.int32)
        out[r] = sol[its * CAP + rank]


def per_device(factor_blocks, pattern, levels, diag_inverse, right_side):
    rhs = jnp.swapaxes(right_side, 1, 2)
    bf, f32, dma = jnp.bfloat16, jnp.float32, pltpu.SemaphoreType.DMA
    vmem = pltpu.VMEM
    out = pl.pallas_call(
        kernel,
        out_shape=jax.ShapeDtypeStruct((ROWS, W, B), f32),
        in_specs=[
            pl.BlockSpec(memory_space=pl.ANY),
            pl.BlockSpec(memory_space=pltpu.SMEM),
            pl.BlockSpec(memory_space=pltpu.SMEM),
            pl.BlockSpec(memory_space=pl.ANY),
            pl.BlockSpec(memory_space=pltpu.VMEM),
        ],
        out_specs=pl.BlockSpec(memory_space=pltpu.VMEM),
        scratch_shapes=[
            vmem((ROWS, 4, SLOTS, B, B), bf),
            vmem((ROWS - EARLY, 4, SLOTS, B, B), bf),
            vmem((CAP, B, B), f32),
            vmem((ROWS, B, B), f32),
            pltpu.SMEM((3, ROWS, SLOTS), jnp.int32),
            vmem((EMPTY + 1, W, B), bf),
            vmem((2, 2, 4, 4, CAP, W, B), bf),
            vmem((LEV * CAP, W, B), f32),
            pltpu.SMEM((CAP * 4 * SLOTS,), jnp.int32),
            pltpu.SMEM((CAP,), jnp.int32),
            dma((4,)), dma((ROWS - EARLY,)), dma((3,)), dma((3,)),
            dma((ROWS, 3)), dma((ROWS, 3)),
            dma((2, 4, 4)), dma((2, 4, 4)), dma((2, 4)), dma((2, 4)),
        ],
        compiler_params=pltpu.CompilerParams(
            collective_id=0, has_side_effects=True, vmem_limit_bytes=56 * 1024 * 1024
        ),
    )(factor_blocks, pattern, levels, diag_inverse, rhs)
    return jnp.swapaxes(out, 1, 2)


def solution(mesh):
    return jax.shard_map(
        per_device,
        mesh=mesh,
        in_specs=(
            P("row", "col", None, None),
            P("row", "col"),
            P(),
            P("row", None, None),
            P("row", None, "col"),
        ),
        out_specs=P("row", None, "col"),
        check_vma=False,
    )
```

```python
import jax
import jax.numpy as jnp
from jax import lax
from jax.experimental import pallas as pl
from jax.experimental.pallas import tpu as pltpu
from jax.sharding import PartitionSpec as P

MESH = pl.DeviceIdType.MESH
LEV = 8
CAP = 3
B = 128
W = 32
ROWS = 16
SLOTS = 5
EMPTY = (LEV - 1) * 32 * CAP
EARLY = 6
AHEAD = 2


def dot_t(a, b):
    return lax.dot_general(a, b, (((1,), (1,)), ((), ())), preferred_element_type=jnp.float32)


def split(a):
    high = a.astype(jnp.bfloat16)
    return high, (a - high.astype(jnp.float32)).astype(jnp.bfloat16)


def times_inverse(v, d):
    n = v.shape[0]
    v_high, v_low = split(v)
    d_high, d_low = split(d)
    both = dot_t(jnp.concatenate([v_high, v_low], axis=0), d_high)
    return both[:n] + (both[n:] + dot_t(v_high, d_low))


def kernel(
    factor, pattern, levels, inverse, rhs, out,
    blocks, late, inv0, inv, pats, table, land, sol, lookup, rows,
    local_sem, late_sem, pat_s, pat_r, zs, zr, gs, gr, cs, cr,
):
    row, z = lax.axis_index("row"), lax.axis_index("col")
    x, y, q = row // 8, lax.rem(row // 2, 4), lax.rem(row, 2)
    chip = x * 4 + y
    partner = (chip * 2 + 1 - q, z)

    def along_z(by):
        return (row, lax.rem(z + by, 4))

    def remote(src, dst, s, r, to):
        return pltpu.make_async_remote_copy(
            src_ref=src, dst_ref=dst, send_sem=s, recv_sem=r, device_id=to, device_id_type=MESH
        )

    own = [
        pltpu.make_async_copy(inverse.at[0:CAP], inv0, local_sem.at[0]),
        pltpu.make_async_copy(inverse, inv, local_sem.at[1]),
        pltpu.make_async_copy(factor.at[0:EARLY], blocks.at[0:EARLY, z], local_sem.at[2]),
        pltpu.make_async_copy(factor.at[EARLY:ROWS], late.at[:, z], local_sem.at[3]),
    ]
    for c in own:
        c.start()

    offsets = [(dx, dy) for dx in range(4) for dy in range(4) if (dx, dy) != (0, 0)]
    offsets.sort(key=lambda o: -(min(o[0], 4 - o[0]) + min(o[1], 4 - o[1])))

    def in_plane(dx, dy):
        return ((lax.rem(x + dx, 4) * 4 + lax.rem(y + dy, 4)) * 2 + q, z)

    barrier = pltpu.get_barrier_semaphore()
    greeted = [partner] + [along_z(by) for by in (1, 2, 3)] + [in_plane(*o) for o in offsets]
    for to in greeted:
        pl.semaphore_signal(barrier, inc=1, device_id=to, device_id_type=MESH)
    table[EMPTY] = jnp.zeros(table.shape[1:], table.dtype)
    pl.semaphore_wait(barrier, len(greeted))

    def home(t, owner):
        if isinstance(t, int) and t < EARLY:
            return blocks.at[t, owner]
        return late.at[t - EARLY, owner]

    def direct(t):
        return [remote(factor.at[t], home(t, z), zs.at[t, k], zr.at[t, k], along_z(1 + 2 * k)) for k in range(2)]

    def arrives(t, k, owner):
        unit = home(t, owner)
        return remote(unit, unit, zs.at[t, k], zr.at[t, k], along_z(1))

    def forward(t):
        by = 1 + 2 * lax.rem(t + q, 2)
        unit = home(t, lax.rem(z + 4 - by, 4))
        return remote(unit, unit, zs.at[t, 2], zr.at[t, 2], along_z(by))

    def pass_on(t):
        k = lax.rem(t + q, 2)
        arrives(t, k, lax.rem(z + 3 - 2 * k, 4)).wait_recv()
        forward(t).start()

    def send_ahead(t):
        for copy in direct(t):
            copy.start()

    def arrive(t):
        k = lax.rem(t + q, 2)
        arrives(t, 1 - k, lax.rem(z + 1 + 2 * k, 4)).wait_recv()
        arrives(t, 2, lax.rem(z + 2, 4)).wait_recv()

    def pattern_copies():
        return [remote(pattern, pats.at[3 - by], pat_s.at[by - 1], pat_r.at[by - 1], along_z(by)) for by in (1, 2, 3)]

    def pattern_arrives():
        return [remote(pats.at[3 - by], pats.at[3 - by], pat_s.at[by - 1], pat_r.at[by - 1], along_z(by)) for by in (1, 2, 3)]

    for copy in pattern_copies():
        copy.start()
    for t in range(1, 1 + AHEAD):
        send_ahead(t)

    def spread(p, dx, dy):
        unit = land.at[p, q, x, y]
        return remote(unit, unit, gs.at[p, dx, dy], gr.at[p, dx, dy], in_plane(dx, dy))

    def spread_in(p, dx, dy):
        unit = land.at[p, q, lax.rem(x + 4 - dx, 4), lax.rem(y + 4 - dy, 4)]
        return remote(unit, unit, gs.at[p, dx, dy], gr.at[p, dx, dy], in_plane(dx, dy))

    def across(p, dx, core):
        unit = land.at[p, core, lax.rem(x + 4 - dx, 4)]
        return remote(unit, unit, cs.at[p, dx], cr.at[p, dx], partner)

    def start_spread(p):
        for o in offsets:
            spread(p, *o).start()

    own[0].wait()
    for c in range(CAP):
        v = times_inverse(rhs[c], inv0[c])
        sol[c] = v
        land[0, q, x, y, c] = v.astype(jnp.bfloat16)
    start_spread(0)

    def find(level):
        first = row * ROWS
        start = jnp.int32(0)
        for r in range(ROWS):
            start += (levels[first + r] < level).astype(jnp.int32)
        for c in range(CAP):
            r = jnp.minimum(start + c, ROWS - 1)
            rows[c] = r
            for k in range(4 * SLOTS):
                far, slot = k // SLOTS, k % SLOTS
                j = pattern[r, slot] if far == 0 else pats[far - 1, r, slot]
                j0 = jnp.maximum(j, 0)
                inside = lax.rem(j0, ROWS)
                its = levels[j0]
                rank = ((levels[jnp.maximum(j0 - 1, 0)] == its) & (inside >= 1)).astype(jnp.int32) + (
                    (levels[jnp.maximum(j0 - 2, 0)] == its) & (inside >= 2)
                ).astype(jnp.int32)
                group = j0 // ROWS
                at = ((its * 2 + lax.rem(group, 2)) * 16 + group // 2) * CAP + rank
                lookup[c * 4 * SLOTS + k] = jnp.where(j < 0, EMPTY, jnp.minimum(at, EMPTY))

    def from_late(t):
        return pltpu.make_async_copy(late.at[t - EARLY], blocks.at[t], late_sem.at[t - EARLY])

    def body(level, carry):
        p = lax.rem(level - 1, 2)
        p_next = lax.rem(level, 2)

        @pl.when(level == 1)
        def _():
            pass_on(1)
            send_ahead(1 + AHEAD)
            for copy in pattern_arrives():
                copy.wait_recv()
            for copy in pattern_copies():
                copy.wait_send()

        find(level)

        @pl.when((level == 2) | (level == 3))
        def _():
            pass_on(3 * level)

        @pl.when((level == 4) | (level == 5))
        def _():
            pass_on(2 * level + 4)

        @pl.when(level == 4)
        def _():
            send_ahead(jnp.int32(14))

        for dx in (0, 1, 3, 2):
            for dy in (1, 3, 2, 0):
                if (dx, dy) != (0, 0):
                    spread_in(p, dx, dy).wait_recv()
            across(p, dx, q).start()

        @pl.when(level == 1)
        def _():
            for t in range(2, EARLY):
                pass_on(t)
                if t + AHEAD < EARLY:
                    send_ahead(t + AHEAD)
            send_ahead(EARLY)
            for t in range(1, EARLY):
                arrive(t)
            send_ahead(EARLY + 1)
            send_ahead(EARLY + 2)
            for copy in own[1:]:
                copy.wait()

        @pl.when((level == 2) | (level == 3))
        def _():
            for i in (1, 2):
                pass_on(3 * level + i)
            send_ahead(3 * level + 3)
            for i in range(3):
                arrive(3 * level + i)
                from_late(3 * level + i).start()
            send_ahead(3 * level + 4)

            @pl.when(level == 2)
            def _():
                send_ahead(jnp.int32(11))

        @pl.when((level == 4) | (level == 5))
        def _():
            pass_on(2 * level + 5)

        @pl.when(level == 4)
        def _():
            send_ahead(jnp.int32(15))

        @pl.when(level >= 4)
        def _():
            arrive(level + 8)
            from_late(level + 8).start()

        for o in offsets:
            spread(p, *o).wait_send()
        for dx in range(4):
            across(p, dx, q).wait_send()
            across(p, dx, 1 - q).wait_recv()

        def to_table(i, carry):
            a, b = i // 4, lax.rem(i, 4)
            for core in range(2):
                for c in range(CAP):
                    table[(((level - 1) * 2 + core) * 16 + i) * CAP + c] = land[p, core, a, b, c]
            return carry

        lax.fori_loop(0, 16, to_table, 0)

        @pl.when((level == 2) | (level == 3))
        def _():
            for i in range(3):
                from_late(3 * level + i).wait()

        @pl.when(level >= 4)
        def _():
            from_late(level + 8).wait()

        for c in range(CAP):
            r = rows[c]
            total = None
            for k in range(0, 4 * SLOTS, 2):
                pieces = [table[lookup[c * 4 * SLOTS + k + i]] for i in range(2)]
                factors = [blocks[r, lax.rem(z + (k + i) // SLOTS, 4), (k + i) % SLOTS] for i in range(2)]
                term = dot_t(jnp.concatenate(pieces, axis=1), jnp.concatenate(factors, axis=1))
                total = term if total is None else total + term
            v = times_inverse(rhs[r] - total, inv[r])
            sol[level * CAP + c] = v
            land[p_next, q, x, y, c] = v.astype(jnp.bfloat16)

        @pl.when(level < LEV - 1)
        def _():
            start_spread(p_next)

        return carry

    lax.fori_loop(1, LEV, body, 0)

    for t in range(1, ROWS):
        for copy in direct(t) + [forward(t)]:
            copy.wait_send()
    for r in range(ROWS):
        its = levels[row * ROWS + r]
        rank = jnp.int32(0)
        for back in (1, 2):
            if r >= back:
                rank += (levels[row * ROWS + r - back] == its).astype(jnp.int32)
        out[r] = sol[its * CAP + rank]


def per_device(factor_blocks, pattern, levels, diag_inverse, right_side):
    rhs = jnp.swapaxes(right_side, 1, 2)
    bf, f32, dma = jnp.bfloat16, jnp.float32, pltpu.SemaphoreType.DMA
    vmem = pltpu.VMEM
    out = pl.pallas_call(
        kernel,
        out_shape=jax.ShapeDtypeStruct((ROWS, W, B), f32),
        in_specs=[
            pl.BlockSpec(memory_space=pl.ANY),
            pl.BlockSpec(memory_space=pltpu.SMEM),
            pl.BlockSpec(memory_space=pltpu.SMEM),
            pl.BlockSpec(memory_space=pl.ANY),
            pl.BlockSpec(memory_space=pltpu.VMEM),
        ],
        out_specs=pl.BlockSpec(memory_space=pltpu.VMEM),
        scratch_shapes=[
            vmem((ROWS, 4, SLOTS, B, B), bf),
            vmem((ROWS - EARLY, 4, SLOTS, B, B), bf),
            vmem((CAP, B, B), f32),
            vmem((ROWS, B, B), f32),
            pltpu.SMEM((3, ROWS, SLOTS), jnp.int32),
            vmem((EMPTY + 1, W, B), bf),
            vmem((2, 2, 4, 4, CAP, W, B), bf),
            vmem((LEV * CAP, W, B), f32),
            pltpu.SMEM((CAP * 4 * SLOTS,), jnp.int32),
            pltpu.SMEM((CAP,), jnp.int32),
            dma((4,)), dma((ROWS - EARLY,)), dma((3,)), dma((3,)),
            dma((ROWS, 3)), dma((ROWS, 3)),
            dma((2, 4, 4)), dma((2, 4, 4)), dma((2, 4)), dma((2, 4)),
        ],
        compiler_params=pltpu.CompilerParams(
            collective_id=0, has_side_effects=True, vmem_limit_bytes=56 * 1024 * 1024
        ),
    )(factor_blocks, pattern, levels, diag_inverse, rhs)
    return jnp.swapaxes(out, 1, 2)


def solution(mesh):
    return jax.shard_map(
        per_device,
        mesh=mesh,
        in_specs=(
            P("row", "col", None, None),
            P("row", "col"),
            P(),
            P("row", None, None),
            P("row", None, "col"),
        ),
        out_specs=P("row", None, "col"),
        check_vma=False,
    )
```

```python
import jax
import jax.numpy as jnp
from jax import lax
from jax.experimental import pallas as pl
from jax.experimental.pallas import tpu as pltpu
from jax.sharding import PartitionSpec as P

MESH = pl.DeviceIdType.MESH
LEV = 8
CAP = 3
B = 128
W = 32
ROWS = 16
SLOTS = 5
EMPTY = (LEV - 1) * 32 * CAP
SENT = ROWS - 1
EARLY = 3
AHEAD = 2


def dot_t(a, b):
    return lax.dot_general(a, b, (((1,), (1,)), ((), ())), preferred_element_type=jnp.float32)


def split(a):
    high = a.astype(jnp.bfloat16)
    return high, (a - high.astype(jnp.float32)).astype(jnp.bfloat16)


def both_terms(d):
    return jnp.concatenate(split(d), axis=0)


def times_inverse(v, d):
    n = v.shape[0]
    v_high, v_low = split(v)
    terms = dot_t(jnp.concatenate([v_high, v_low], axis=0), d)
    return terms[:n, :B] + (terms[n:, :B] + terms[:n, B:])


def kernel(
    factor, pattern, levels, inverse, right, out,
    raw, blocks, late, inv0, inv, inv_terms, right_in, rhs, pats, table, land, sol, lookup, rows, places,
    local_sem, late_sem, pat_s, pat_r, zs, zr, gs, gr, cs, cr,
):
    row, z = lax.axis_index("row"), lax.axis_index("col")
    x, y, q = row // 8, lax.rem(row // 2, 4), lax.rem(row, 2)
    chip = x * 4 + y
    partner = (chip * 2 + 1 - q, z)

    def along_z(by):
        return (row, lax.rem(z + by, 4))

    def remote(src, dst, s, r, to):
        return pltpu.make_async_remote_copy(
            src_ref=src, dst_ref=dst, send_sem=s, recv_sem=r, device_id=to, device_id_type=MESH
        )

    own = [
        pltpu.make_async_copy(inverse.at[0:CAP], inv0, local_sem.at[0]),
        pltpu.make_async_copy(inverse, inv, local_sem.at[1]),
        pltpu.make_async_copy(factor, raw, local_sem.at[2]),
        pltpu.make_async_copy(right.at[0:CAP], right_in.at[0:CAP], local_sem.at[3]),
        pltpu.make_async_copy(right.at[CAP:ROWS], right_in.at[CAP:ROWS], local_sem.at[4]),
    ]
    for i in (0, 3, 2, 1, 4):
        own[i].start()

    offsets = [(dx, dy) for dx in range(4) for dy in range(4) if (dx, dy) != (0, 0)]
    offsets.sort(key=lambda o: -(min(o[0], 4 - o[0]) + min(o[1], 4 - o[1])))

    def in_plane(dx, dy):
        return ((lax.rem(x + dx, 4) * 4 + lax.rem(y + dy, 4)) * 2 + q, z)

    barrier = pltpu.get_barrier_semaphore()
    greeted = [partner] + [along_z(by) for by in (1, 2, 3)] + [in_plane(*o) for o in offsets]
    for to in greeted:
        pl.semaphore_signal(barrier, inc=1, device_id=to, device_id_type=MESH)
    table[EMPTY] = jnp.zeros(table.shape[1:], table.dtype)

    def count_below(level):
        count = jnp.int32(0)
        for r in range(ROWS):
            count += (levels[row * ROWS + r] < level).astype(jnp.int32)
        return count

    skipped = count_below(1)
    own[3].wait()
    for r in range(CAP):
        rhs[r] = jnp.swapaxes(right_in[r], 0, 1)
    own[2].wait()
    for n in range(EARLY):
        blocks[n, z] = raw[jnp.minimum(skipped + n, ROWS - 1)]

    def shift(n, carry):
        late[n - EARLY, z] = raw[jnp.minimum(skipped + n, ROWS - 1)]
        return carry

    lax.fori_loop(EARLY, SENT, shift, 0)
    pl.semaphore_wait(barrier, len(greeted))

    def home(t, owner):
        if isinstance(t, int) and t < EARLY:
            return blocks.at[t, owner]
        return late.at[t - EARLY, owner]

    def direct(t):
        return [remote(home(t, z), home(t, z), zs.at[t, k], zr.at[t, k], along_z(1 + 2 * k)) for k in range(2)]

    def arrives(t, k, owner):
        unit = home(t, owner)
        return remote(unit, unit, zs.at[t, k], zr.at[t, k], along_z(1))

    def forward(t):
        by = 1 + 2 * lax.rem(t + q, 2)
        unit = home(t, lax.rem(z + 4 - by, 4))
        return remote(unit, unit, zs.at[t, 2], zr.at[t, 2], along_z(by))

    def pass_on(t):
        k = lax.rem(t + q, 2)
        arrives(t, k, lax.rem(z + 3 - 2 * k, 4)).wait_recv()
        forward(t).start()

    def send_ahead(t):
        for copy in direct(t):
            copy.start()

    def arrive(t):
        k = lax.rem(t + q, 2)
        arrives(t, 1 - k, lax.rem(z + 1 + 2 * k, 4)).wait_recv()
        arrives(t, 2, lax.rem(z + 2, 4)).wait_recv()

    def pattern_copies():
        return [remote(pattern, pats.at[3 - by], pat_s.at[by - 1], pat_r.at[by - 1], along_z(by)) for by in (1, 2, 3)]

    def pattern_arrives():
        return [remote(pats.at[3 - by], pats.at[3 - by], pat_s.at[by - 1], pat_r.at[by - 1], along_z(by)) for by in (1, 2, 3)]

    for copy in pattern_copies():
        copy.start()
    for t in range(AHEAD):
        send_ahead(t)

    def spread(p, dx, dy):
        unit = land.at[p, q, x, y]
        return remote(unit, unit, gs.at[p, dx, dy], gr.at[p, dx, dy], in_plane(dx, dy))

    def spread_in(p, dx, dy):
        unit = land.at[p, q, lax.rem(x + 4 - dx, 4), lax.rem(y + 4 - dy, 4)]
        return remote(unit, unit, gs.at[p, dx, dy], gr.at[p, dx, dy], in_plane(dx, dy))

    def across(p, dx, core):
        unit = land.at[p, core, lax.rem(x + 4 - dx, 4)]
        return remote(unit, unit, cs.at[p, dx], cr.at[p, dx], partner)

    def start_spread(p):
        for o in offsets:
            spread(p, *o).start()

    own[0].wait()
    for c in range(CAP):
        v = times_inverse(rhs[c], both_terms(inv0[c]))
        sol[c] = v
        land[0, q, x, y, c] = v.astype(jnp.bfloat16)
    start_spread(0)
    own[1].wait()
    own[4].wait()

    def prepare(r, carry):
        inv_terms[r] = both_terms(inv[r])
        rhs[r] = jnp.swapaxes(right_in[r], 0, 1)
        return carry

    lax.fori_loop(0, ROWS, prepare, 0)

    def find(level):
        start = count_below(level)
        for c in range(CAP):
            r = jnp.minimum(start + c, ROWS - 1)
            rows[c] = r
            places[c] = jnp.clip(r - skipped, 0, SENT - 1)
            for k in range(4 * SLOTS):
                far, slot = k // SLOTS, k % SLOTS
                j = pattern[r, slot] if far == 0 else pats[far - 1, r, slot]
                j0 = jnp.maximum(j, 0)
                inside = lax.rem(j0, ROWS)
                its = levels[j0]
                rank = ((levels[jnp.maximum(j0 - 1, 0)] == its) & (inside >= 1)).astype(jnp.int32) + (
                    (levels[jnp.maximum(j0 - 2, 0)] == its) & (inside >= 2)
                ).astype(jnp.int32)
                group = j0 // ROWS
                at = ((its * 2 + lax.rem(group, 2)) * 16 + group // 2) * CAP + rank
                lookup[c * 4 * SLOTS + k] = jnp.where(j < 0, EMPTY, jnp.minimum(at, EMPTY))

    def from_late(t):
        return pltpu.make_async_copy(late.at[t - EARLY], blocks.at[t], late_sem.at[t - EARLY])

    def body(level, carry):
        p = lax.rem(level - 1, 2)
        p_next = lax.rem(level, 2)

        @pl.when(level == 1)
        def _():
            pass_on(0)
            send_ahead(AHEAD)
            for copy in pattern_arrives():
                copy.wait_recv()
            for copy in pattern_copies():
                copy.wait_send()

        find(level)

        @pl.when((level >= 2) & (level <= 4))
        def _():
            pass_on(3 * level - 3)

        @pl.when((level == 5) | (level == 6))
        def _():
            pass_on(2 * level + 2)

        for dx in (0, 1, 3, 2):
            for dy in (1, 3, 2, 0):
                if (dx, dy) != (0, 0):
                    spread_in(p, dx, dy).wait_recv()
            across(p, dx, q).start()

        @pl.when(level == 1)
        def _():
            for t in range(1, EARLY):
                pass_on(t)
            send_ahead(EARLY)
            for t in range(EARLY):
                arrive(t)
            send_ahead(EARLY + 1)
            send_ahead(EARLY + 2)

        @pl.when((level >= 2) & (level <= 4))
        def _():
            for i in (1, 2):
                pass_on(3 * level - 3 + i)
            send_ahead(3 * level)
            for i in range(3):
                arrive(3 * level - 3 + i)
                from_late(3 * level - 3 + i).start()
            send_ahead(3 * level + 1)
            send_ahead(3 * level + 2)

        @pl.when(level == 5)
        def _():
            pass_on(jnp.int32(13))

        @pl.when(level >= 5)
        def _():
            arrive(level + 7)
            from_late(level + 7).start()

        for o in offsets:
            spread(p, *o).wait_send()
        for dx in range(4):
            across(p, dx, q).wait_send()
            across(p, dx, 1 - q).wait_recv()

        def to_table(i, carry):
            a, b = i // 4, lax.rem(i, 4)
            for core in range(2):
                for c in range(CAP):
                    table[(((level - 1) * 2 + core) * 16 + i) * CAP + c] = land[p, core, a, b, c]
            return carry

        lax.fori_loop(0, 16, to_table, 0)

        @pl.when((level >= 2) & (level <= 4))
        def _():
            for i in range(3):
                from_late(3 * level - 3 + i).wait()

        @pl.when(level >= 5)
        def _():
            from_late(level + 7).wait()

        for c in range(CAP):
            r = rows[c]
            total = None
            for k in range(0, 4 * SLOTS, 2):
                pieces = [table[lookup[c * 4 * SLOTS + k + i]] for i in range(2)]
                factors = [blocks[places[c], lax.rem(z + (k + i) // SLOTS, 4), (k + i) % SLOTS] for i in range(2)]
                term = dot_t(jnp.concatenate(pieces, axis=1), jnp.concatenate(factors, axis=1))
                total = term if total is None else total + term
            v = times_inverse(rhs[r] - total, inv_terms[r])
            sol[level * CAP + c] = v
            land[p_next, q, x, y, c] = v.astype(jnp.bfloat16)

        @pl.when(level < LEV - 1)
        def _():
            start_spread(p_next)

        return carry

    lax.fori_loop(1, LEV, body, 0)

    for t in range(SENT):
        for copy in direct(t) + [forward(t)]:
            copy.wait_send()
    for r in range(ROWS):
        its = levels[row * ROWS + r]
        rank = jnp.int32(0)
        for back in (1, 2):
            if r >= back:
                rank += (levels[row * ROWS + r - back] == its).astype(jnp.int32)
        out[r] = sol[its * CAP + rank]


def per_device(factor_blocks, pattern, levels, diag_inverse, right_side):
    bf, f32, dma = jnp.bfloat16, jnp.float32, pltpu.SemaphoreType.DMA
    vmem = pltpu.VMEM
    out = pl.pallas_call(
        kernel,
        out_shape=jax.ShapeDtypeStruct((ROWS, W, B), f32),
        in_specs=[
            pl.BlockSpec(memory_space=pl.ANY),
            pl.BlockSpec(memory_space=pltpu.SMEM),
            pl.BlockSpec(memory_space=pltpu.SMEM),
            pl.BlockSpec(memory_space=pl.ANY),
            pl.BlockSpec(memory_space=pl.ANY),
        ],
        out_specs=pl.BlockSpec(memory_space=pltpu.VMEM),
        scratch_shapes=[
            vmem((ROWS, SLOTS, B, B), bf),
            vmem((SENT, 4, SLOTS, B, B), bf),
            vmem((SENT - EARLY, 4, SLOTS, B, B), bf),
            vmem((CAP, B, B), f32),
            vmem((ROWS, B, B), f32),
            vmem((ROWS, 2 * B, B), bf),
            vmem((ROWS, B, W), f32),
            vmem((ROWS, W, B), f32),
            pltpu.SMEM((3, ROWS, SLOTS), jnp.int32),
            vmem((EMPTY + 1, W, B), bf),
            vmem((2, 2, 4, 4, CAP, W, B), bf),
            vmem((LEV * CAP, W, B), f32),
            pltpu.SMEM((CAP * 4 * SLOTS,), jnp.int32),
            pltpu.SMEM((CAP,), jnp.int32),
            pltpu.SMEM((CAP,), jnp.int32),
            dma((5,)), dma((SENT - EARLY,)), dma((3,)), dma((3,)),
            dma((SENT, 3)), dma((SENT, 3)),
            dma((2, 4, 4)), dma((2, 4, 4)), dma((2, 4)), dma((2, 4)),
        ],
        compiler_params=pltpu.CompilerParams(
            collective_id=0, has_side_effects=True, vmem_limit_bytes=56 * 1024 * 1024
        ),
    )(factor_blocks, pattern, levels, diag_inverse, right_side)
    return jnp.swapaxes(out, 1, 2)


def solution(mesh):
    return jax.shard_map(
        per_device,
        mesh=mesh,
        in_specs=(
            P("row", "col", None, None),
            P("row", "col"),
            P(),
            P("row", None, None),
            P("row", None, "col"),
        ),
        out_specs=P("row", None, "col"),
        check_vma=False,
    )
```

```python
import jax
import jax.numpy as jnp
from jax import lax
from jax.experimental import pallas as pl
from jax.experimental.pallas import tpu as pltpu
from jax.sharding import PartitionSpec as P

MESH = pl.DeviceIdType.MESH
LEV = 8
CAP = 3
B = 128
W = 32
ROWS = 16
SLOTS = 5
EMPTY = (LEV - 1) * 32 * CAP
SENT = ROWS - 1
EARLY = 3
AHEAD = 2


def dot_t(a, b):
    return lax.dot_general(a, b, (((1,), (1,)), ((), ())), preferred_element_type=jnp.float32)


def split(a):
    high = a.astype(jnp.bfloat16)
    return high, (a - high.astype(jnp.float32)).astype(jnp.bfloat16)


def both_terms(d):
    return jnp.concatenate(split(d), axis=0)


def times_inverse(v, d):
    n = v.shape[0]
    v_high, v_low = split(v)
    terms = dot_t(jnp.concatenate([v_high, v_low], axis=0), d)
    return terms[:n, :B] + (terms[n:, :B] + terms[:n, B:])


def kernel(
    factor, pattern, levels, inverse, right, out,
    raw, blocks, late, inv0, inv, inv_terms, rhs, pats, table, land, sol, lookup, rows, places,
    local_sem, late_sem, pat_s, pat_r, zs, zr, gs, gr, cs, cr,
):
    row, z = lax.axis_index("row"), lax.axis_index("col")
    x, y, q = row // 8, lax.rem(row // 2, 4), lax.rem(row, 2)
    chip = x * 4 + y
    partner = (chip * 2 + 1 - q, z)

    def along_z(by):
        return (row, lax.rem(z + by, 4))

    def remote(src, dst, s, r, to):
        return pltpu.make_async_remote_copy(
            src_ref=src, dst_ref=dst, send_sem=s, recv_sem=r, device_id=to, device_id_type=MESH
        )

    own = [
        pltpu.make_async_copy(inverse.at[0:CAP], inv0, local_sem.at[0]),
        pltpu.make_async_copy(inverse, inv, local_sem.at[1]),
        pltpu.make_async_copy(factor, raw, local_sem.at[2]),
        pltpu.make_async_copy(right.at[0:CAP], rhs.at[0:CAP], local_sem.at[3]),
        pltpu.make_async_copy(right.at[CAP:ROWS], rhs.at[CAP:ROWS], local_sem.at[4]),
    ]
    for i in (2, 0, 3, 1, 4):
        own[i].start()

    offsets = [(dx, dy) for dx in range(4) for dy in range(4) if (dx, dy) != (0, 0)]
    offsets.sort(key=lambda o: -(min(o[0], 4 - o[0]) + min(o[1], 4 - o[1])))

    def in_plane(dx, dy):
        return ((lax.rem(x + dx, 4) * 4 + lax.rem(y + dy, 4)) * 2 + q, z)

    barrier = pltpu.get_barrier_semaphore()
    greeted = [partner] + [along_z(by) for by in (1, 2, 3)] + [in_plane(*o) for o in offsets]
    for to in greeted:
        pl.semaphore_signal(barrier, inc=1, device_id=to, device_id_type=MESH)
    table[EMPTY] = jnp.zeros(table.shape[1:], table.dtype)

    def count_below(level):
        count = jnp.int32(0)
        for r in range(ROWS):
            count += (levels[row * ROWS + r] < level).astype(jnp.int32)
        return count

    skipped = count_below(1)
    own[2].wait()
    for n in range(EARLY):
        blocks[n, z] = raw[jnp.minimum(skipped + n, ROWS - 1)]

    def shift(n, carry):
        late[n - EARLY, z] = raw[jnp.minimum(skipped + n, ROWS - 1)]
        return carry

    lax.fori_loop(EARLY, SENT, shift, 0)
    pl.semaphore_wait(barrier, len(greeted))

    def home(t, owner):
        if isinstance(t, int) and t < EARLY:
            return blocks.at[t, owner]
        return late.at[t - EARLY, owner]

    def direct(t):
        return [remote(home(t, z), home(t, z), zs.at[t, k], zr.at[t, k], along_z(1 + 2 * k)) for k in range(2)]

    def arrives(t, k, owner):
        unit = home(t, owner)
        return remote(unit, unit, zs.at[t, k], zr.at[t, k], along_z(1))

    def forward(t):
        by = 1 + 2 * lax.rem(t + q, 2)
        unit = home(t, lax.rem(z + 4 - by, 4))
        return remote(unit, unit, zs.at[t, 2], zr.at[t, 2], along_z(by))

    def pass_on(t):
        k = lax.rem(t + q, 2)
        arrives(t, k, lax.rem(z + 3 - 2 * k, 4)).wait_recv()
        forward(t).start()

    def send_ahead(t):
        for copy in direct(t):
            copy.start()

    def arrive(t):
        k = lax.rem(t + q, 2)
        arrives(t, 1 - k, lax.rem(z + 1 + 2 * k, 4)).wait_recv()
        arrives(t, 2, lax.rem(z + 2, 4)).wait_recv()

    def pattern_copies():
        return [remote(pattern, pats.at[3 - by], pat_s.at[by - 1], pat_r.at[by - 1], along_z(by)) for by in (1, 2, 3)]

    def pattern_arrives():
        return [remote(pats.at[3 - by], pats.at[3 - by], pat_s.at[by - 1], pat_r.at[by - 1], along_z(by)) for by in (1, 2, 3)]

    for copy in pattern_copies():
        copy.start()
    for t in range(AHEAD):
        send_ahead(t)

    def spread(p, dx, dy):
        unit = land.at[p, q, x, y]
        return remote(unit, unit, gs.at[p, dx, dy], gr.at[p, dx, dy], in_plane(dx, dy))

    def spread_in(p, dx, dy):
        unit = land.at[p, q, lax.rem(x + 4 - dx, 4), lax.rem(y + 4 - dy, 4)]
        return remote(unit, unit, gs.at[p, dx, dy], gr.at[p, dx, dy], in_plane(dx, dy))

    def across(p, dx, core):
        unit = land.at[p, core, lax.rem(x + 4 - dx, 4)]
        return remote(unit, unit, cs.at[p, dx], cr.at[p, dx], partner)

    def start_spread(p):
        for o in offsets:
            spread(p, *o).start()

    own[0].wait()
    own[3].wait()
    for c in range(CAP):
        v = times_inverse(rhs[c], both_terms(inv0[c]))
        sol[c] = v
        land[0, q, x, y, c] = v.astype(jnp.bfloat16)
    start_spread(0)
    own[1].wait()
    own[4].wait()

    def prepare(r, carry):
        inv_terms[r] = both_terms(inv[r])
        return carry

    lax.fori_loop(0, ROWS, prepare, 0)

    def find(level):
        start = count_below(level)
        for c in range(CAP):
            r = jnp.minimum(start + c, ROWS - 1)
            rows[c] = r
            places[c] = jnp.clip(r - skipped, 0, SENT - 1)
            for k in range(4 * SLOTS):
                far, slot = k // SLOTS, k % SLOTS
                j = pattern[slot, r] if far == 0 else pats[far - 1, slot, r]
                j0 = jnp.maximum(j, 0)
                inside = lax.rem(j0, ROWS)
                its = levels[j0]
                rank = ((levels[jnp.maximum(j0 - 1, 0)] == its) & (inside >= 1)).astype(jnp.int32) + (
                    (levels[jnp.maximum(j0 - 2, 0)] == its) & (inside >= 2)
                ).astype(jnp.int32)
                group = j0 // ROWS
                at = ((its * 2 + lax.rem(group, 2)) * 16 + group // 2) * CAP + rank
                lookup[c * 4 * SLOTS + k] = jnp.where(j < 0, EMPTY, jnp.minimum(at, EMPTY))

    def from_late(t):
        return pltpu.make_async_copy(late.at[t - EARLY], blocks.at[t], late_sem.at[t - EARLY])

    def body(level, carry):
        p = lax.rem(level - 1, 2)
        p_next = lax.rem(level, 2)

        @pl.when(level == 1)
        def _():
            pass_on(0)
            send_ahead(AHEAD)
            for copy in pattern_arrives():
                copy.wait_recv()
            for copy in pattern_copies():
                copy.wait_send()

        find(level)

        @pl.when((level >= 2) & (level <= 4))
        def _():
            pass_on(3 * level - 3)

        @pl.when((level == 5) | (level == 6))
        def _():
            pass_on(2 * level + 2)

        for dx in (0, 1, 3, 2):
            for dy in (1, 3, 2, 0):
                if (dx, dy) != (0, 0):
                    spread_in(p, dx, dy).wait_recv()
            across(p, dx, q).start()

        @pl.when(level == 1)
        def _():
            for t in range(1, EARLY):
                pass_on(t)
            send_ahead(EARLY)
            for t in range(EARLY):
                arrive(t)
            send_ahead(EARLY + 1)
            send_ahead(EARLY + 2)

        @pl.when((level >= 2) & (level <= 4))
        def _():
            for i in (1, 2):
                pass_on(3 * level - 3 + i)
            send_ahead(3 * level)
            for i in range(3):
                arrive(3 * level - 3 + i)
                from_late(3 * level - 3 + i).start()
            send_ahead(3 * level + 1)
            send_ahead(3 * level + 2)

        @pl.when(level == 5)
        def _():
            pass_on(jnp.int32(13))

        @pl.when(level >= 5)
        def _():
            arrive(level + 7)
            from_late(level + 7).start()

        for o in offsets:
            spread(p, *o).wait_send()
        for dx in range(4):
            across(p, dx, q).wait_send()
            across(p, dx, 1 - q).wait_recv()

        def to_table(i, carry):
            a, b = i // 4, lax.rem(i, 4)
            for core in range(2):
                for c in range(CAP):
                    table[(((level - 1) * 2 + core) * 16 + i) * CAP + c] = land[p, core, a, b, c]
            return carry

        lax.fori_loop(0, 16, to_table, 0)

        @pl.when((level >= 2) & (level <= 4))
        def _():
            for i in range(3):
                from_late(3 * level - 3 + i).wait()

        @pl.when(level >= 5)
        def _():
            from_late(level + 7).wait()

        for c in range(CAP):
            r = rows[c]
            total = None
            for k in range(0, 4 * SLOTS, 2):
                pieces = [table[lookup[c * 4 * SLOTS + k + i]] for i in range(2)]
                factors = [blocks[places[c], lax.rem(z + (k + i) // SLOTS, 4), (k + i) % SLOTS] for i in range(2)]
                term = dot_t(jnp.concatenate(pieces, axis=1), jnp.concatenate(factors, axis=1))
                total = term if total is None else total + term
            v = times_inverse(rhs[r] - total, inv_terms[r])
            sol[level * CAP + c] = v
            land[p_next, q, x, y, c] = v.astype(jnp.bfloat16)

        @pl.when(level < LEV - 1)
        def _():
            start_spread(p_next)

        return carry

    lax.fori_loop(1, LEV, body, 0)

    for t in range(SENT):
        for copy in direct(t) + [forward(t)]:
            copy.wait_send()
    for r in range(ROWS):
        its = levels[row * ROWS + r]
        rank = jnp.int32(0)
        for back in (1, 2):
            if r >= back:
                rank += (levels[row * ROWS + r - back] == its).astype(jnp.int32)
        out[r] = sol[its * CAP + rank]


def per_device(factor_blocks, pattern, levels, diag_inverse, right_side):
    bf, f32, dma = jnp.bfloat16, jnp.float32, pltpu.SemaphoreType.DMA
    vmem = pltpu.VMEM
    out = pl.pallas_call(
        kernel,
        out_shape=jax.ShapeDtypeStruct((ROWS, W, B), f32),
        in_specs=[
            pl.BlockSpec(memory_space=pl.ANY),
            pl.BlockSpec(memory_space=pltpu.SMEM),
            pl.BlockSpec(memory_space=pltpu.SMEM),
            pl.BlockSpec(memory_space=pl.ANY),
            pl.BlockSpec(memory_space=pl.ANY),
        ],
        out_specs=pl.BlockSpec(memory_space=pltpu.VMEM),
        scratch_shapes=[
            vmem((ROWS, SLOTS, B, B), bf),
            vmem((SENT, 4, SLOTS, B, B), bf),
            vmem((SENT - EARLY, 4, SLOTS, B, B), bf),
            vmem((CAP, B, B), f32),
            vmem((ROWS, B, B), f32),
            vmem((ROWS, 2 * B, B), bf),
            vmem((ROWS, W, B), f32),
            pltpu.SMEM((3, SLOTS, ROWS), jnp.int32),
            vmem((EMPTY + 1, W, B), bf),
            vmem((2, 2, 4, 4, CAP, W, B), bf),
            vmem((LEV * CAP, W, B), f32),
            pltpu.SMEM((CAP * 4 * SLOTS,), jnp.int32),
            pltpu.SMEM((CAP,), jnp.int32),
            pltpu.SMEM((CAP,), jnp.int32),
            dma((5,)), dma((SENT - EARLY,)), dma((3,)), dma((3,)),
            dma((SENT, 3)), dma((SENT, 3)),
            dma((2, 4, 4)), dma((2, 4, 4)), dma((2, 4)), dma((2, 4)),
        ],
        compiler_params=pltpu.CompilerParams(
            collective_id=0, has_side_effects=True, vmem_limit_bytes=56 * 1024 * 1024
        ),
    )(factor_blocks, pattern.T, levels, diag_inverse, jnp.swapaxes(right_side, 1, 2))
    return jnp.swapaxes(out, 1, 2)


def solution(mesh):
    return jax.shard_map(
        per_device,
        mesh=mesh,
        in_specs=(
            P("row", "col", None, None),
            P("row", "col"),
            P(),
            P("row", None, None),
            P("row", None, "col"),
        ),
        out_specs=P("row", None, "col"),
        check_vma=False,
    )
```

```python
import jax
import jax.numpy as jnp
from jax import lax
from jax.experimental import pallas as pl
from jax.experimental.pallas import tpu as pltpu
from jax.sharding import PartitionSpec as P

MESH = pl.DeviceIdType.MESH
LEV = 8
CAP = 3
B = 128
W = 32
ROWS = 16
SLOTS = 5
EMPTY = (LEV - 1) * 32 * CAP
SENT = ROWS - 1
EARLY = 3
AHEAD = 2


def dot_t(a, b):
    return lax.dot_general(a, b, (((1,), (1,)), ((), ())), preferred_element_type=jnp.float32)


def split(a):
    high = a.astype(jnp.bfloat16)
    return high, (a - high.astype(jnp.float32)).astype(jnp.bfloat16)


def both_terms(d):
    return jnp.concatenate(split(d), axis=0)


def times_inverse(v, d):
    n = v.shape[0]
    v_high, v_low = split(v)
    terms = dot_t(jnp.concatenate([v_high, v_low], axis=0), d)
    return terms[:n, :B] + (terms[n:, :B] + terms[:n, B:])


def kernel(
    factor, pattern, levels, inverse, right, out,
    raw, blocks, late, inv0, inv, inv_terms, rhs, pats, table, land, sol, lookup, rows, places,
    local_sem, late_sem, pat_s, pat_r, zs, zr, gs, gr, cs, cr,
):
    row, z = lax.axis_index("row"), lax.axis_index("col")
    x, y, q = row // 8, lax.rem(row // 2, 4), lax.rem(row, 2)
    chip = x * 4 + y
    partner = (chip * 2 + 1 - q, z)

    def along_z(by):
        return (row, lax.rem(z + by, 4))

    def remote(src, dst, s, r, to):
        return pltpu.make_async_remote_copy(
            src_ref=src, dst_ref=dst, send_sem=s, recv_sem=r, device_id=to, device_id_type=MESH
        )

    own = [
        pltpu.make_async_copy(inverse.at[0:CAP], inv0, local_sem.at[0]),
        pltpu.make_async_copy(inverse, inv, local_sem.at[1]),
        pltpu.make_async_copy(factor, raw, local_sem.at[2]),
        pltpu.make_async_copy(right.at[0:CAP], rhs.at[0:CAP], local_sem.at[3]),
        pltpu.make_async_copy(right.at[CAP:ROWS], rhs.at[CAP:ROWS], local_sem.at[4]),
    ]

    offsets = [(dx, dy) for dx in range(4) for dy in range(4) if (dx, dy) != (0, 0)]
    offsets.sort(key=lambda o: -(min(o[0], 4 - o[0]) + min(o[1], 4 - o[1])))

    def in_plane(dx, dy):
        return ((lax.rem(x + dx, 4) * 4 + lax.rem(y + dy, 4)) * 2 + q, z)

    barrier = pltpu.get_barrier_semaphore()
    greeted = [partner] + [along_z(by) for by in (1, 2, 3)] + [in_plane(*o) for o in offsets]
    for to in greeted:
        pl.semaphore_signal(barrier, inc=1, device_id=to, device_id_type=MESH)
    for i in (2, 0, 3, 1, 4):
        own[i].start()
    table[EMPTY] = jnp.zeros(table.shape[1:], table.dtype)

    def count_below(level):
        count = jnp.int32(0)
        for r in range(ROWS):
            count += (levels[row * ROWS + r] < level).astype(jnp.int32)
        return count

    skipped = count_below(1)
    own[2].wait()
    for n in range(EARLY):
        blocks[n, z] = raw[jnp.minimum(skipped + n, ROWS - 1)]

    def shift(n, carry):
        late[n - EARLY, z] = raw[jnp.minimum(skipped + n, ROWS - 1)]
        return carry

    lax.fori_loop(EARLY, SENT, shift, 0)
    pl.semaphore_wait(barrier, len(greeted))

    def home(t, owner):
        if isinstance(t, int) and t < EARLY:
            return blocks.at[t, owner]
        return late.at[t - EARLY, owner]

    def direct(t):
        return [remote(home(t, z), home(t, z), zs.at[t, k], zr.at[t, k], along_z(1 + 2 * k)) for k in range(2)]

    def arrives(t, k, owner):
        unit = home(t, owner)
        return remote(unit, unit, zs.at[t, k], zr.at[t, k], along_z(1))

    def forward(t):
        by = 1 + 2 * lax.rem(t + q, 2)
        unit = home(t, lax.rem(z + 4 - by, 4))
        return remote(unit, unit, zs.at[t, 2], zr.at[t, 2], along_z(by))

    def pass_on(t):
        k = lax.rem(t + q, 2)
        arrives(t, k, lax.rem(z + 3 - 2 * k, 4)).wait_recv()
        forward(t).start()

    def send_ahead(t):
        for copy in direct(t):
            copy.start()

    def arrive(t):
        k = lax.rem(t + q, 2)
        arrives(t, 1 - k, lax.rem(z + 1 + 2 * k, 4)).wait_recv()
        arrives(t, 2, lax.rem(z + 2, 4)).wait_recv()

    def pattern_copies():
        return [remote(pattern, pats.at[3 - by], pat_s.at[by - 1], pat_r.at[by - 1], along_z(by)) for by in (1, 2, 3)]

    def pattern_arrives():
        return [remote(pats.at[3 - by], pats.at[3 - by], pat_s.at[by - 1], pat_r.at[by - 1], along_z(by)) for by in (1, 2, 3)]

    for copy in pattern_copies():
        copy.start()
    for t in range(AHEAD):
        send_ahead(t)

    def spread(p, dx, dy):
        unit = land.at[p, q, x, y]
        return remote(unit, unit, gs.at[p, dx, dy], gr.at[p, dx, dy], in_plane(dx, dy))

    def spread_in(p, dx, dy):
        unit = land.at[p, q, lax.rem(x + 4 - dx, 4), lax.rem(y + 4 - dy, 4)]
        return remote(unit, unit, gs.at[p, dx, dy], gr.at[p, dx, dy], in_plane(dx, dy))

    def across(p, dx, core):
        unit = land.at[p, core, lax.rem(x + 4 - dx, 4)]
        return remote(unit, unit, cs.at[p, dx], cr.at[p, dx], partner)

    def start_spread(p):
        for o in offsets:
            spread(p, *o).start()

    own[0].wait()
    own[3].wait()
    for c in range(CAP):
        v = times_inverse(rhs[c], both_terms(inv0[c]))
        sol[c] = v
        land[0, q, x, y, c] = v.astype(jnp.bfloat16)
    start_spread(0)
    own[1].wait()
    own[4].wait()

    def prepare(r, carry):
        inv_terms[r] = both_terms(inv[r])
        return carry

    lax.fori_loop(0, ROWS, prepare, 0)

    def find(level):
        start = count_below(level)
        for c in range(CAP):
            r = jnp.minimum(start + c, ROWS - 1)
            rows[c] = r
            places[c] = jnp.clip(r - skipped, 0, SENT - 1)
            for k in range(4 * SLOTS):
                far, slot = k // SLOTS, k % SLOTS
                j = pattern[slot, r] if far == 0 else pats[far - 1, slot, r]
                j0 = jnp.maximum(j, 0)
                inside = lax.rem(j0, ROWS)
                its = levels[j0]
                rank = ((levels[jnp.maximum(j0 - 1, 0)] == its) & (inside >= 1)).astype(jnp.int32) + (
                    (levels[jnp.maximum(j0 - 2, 0)] == its) & (inside >= 2)
                ).astype(jnp.int32)
                group = j0 // ROWS
                at = ((its * 2 + lax.rem(group, 2)) * 16 + group // 2) * CAP + rank
                lookup[c * 4 * SLOTS + k] = jnp.where(j < 0, EMPTY, jnp.minimum(at, EMPTY))

    def from_late(t):
        return pltpu.make_async_copy(late.at[t - EARLY], blocks.at[t], late_sem.at[t - EARLY])

    def give(some):
        for r in some:
            its = levels[row * ROWS + r]
            rank = jnp.int32(0)
            for back in (1, 2):
                if r >= back:
                    rank += (levels[row * ROWS + r - back] == its).astype(jnp.int32)
            out[r] = sol[its * CAP + rank]

    def body(level, carry):
        p = lax.rem(level - 1, 2)
        p_next = lax.rem(level, 2)

        @pl.when(level == 1)
        def _():
            pass_on(0)
            send_ahead(AHEAD)
            for copy in pattern_arrives():
                copy.wait_recv()
            for copy in pattern_copies():
                copy.wait_send()

        find(level)

        @pl.when(level == LEV - 1)
        def _():
            give(range(ROWS - CAP))

        @pl.when((level >= 2) & (level <= 4))
        def _():
            pass_on(3 * level - 3)

        @pl.when((level == 5) | (level == 6))
        def _():
            pass_on(2 * level + 2)

        for dx in (0, 1, 3, 2):
            for dy in (1, 3, 2, 0):
                if (dx, dy) != (0, 0):
                    spread_in(p, dx, dy).wait_recv()
            across(p, dx, q).start()

        @pl.when(level == 1)
        def _():
            for t in range(1, EARLY):
                pass_on(t)
            send_ahead(EARLY)
            send_ahead(EARLY + 1)
            for t in range(EARLY):
                arrive(t)
            send_ahead(EARLY + 2)

        @pl.when((level >= 2) & (level <= 4))
        def _():
            for i in (1, 2):
                pass_on(3 * level - 3 + i)
            send_ahead(3 * level)
            for i in range(3):
                arrive(3 * level - 3 + i)
                from_late(3 * level - 3 + i).start()
            send_ahead(3 * level + 1)
            send_ahead(3 * level + 2)

        @pl.when(level == 5)
        def _():
            pass_on(jnp.int32(13))

        @pl.when(level >= 5)
        def _():
            arrive(level + 7)
            from_late(level + 7).start()

        for o in offsets:
            spread(p, *o).wait_send()
        for dx in range(4):
            across(p, dx, q).wait_send()
            across(p, dx, 1 - q).wait_recv()

        def to_table(i, carry):
            a, b = i // 4, lax.rem(i, 4)
            for core in range(2):
                for c in range(CAP):
                    table[(((level - 1) * 2 + core) * 16 + i) * CAP + c] = land[p, core, a, b, c]
            return carry

        lax.fori_loop(0, 16, to_table, 0)

        @pl.when((level >= 2) & (level <= 4))
        def _():
            for i in range(3):
                from_late(3 * level - 3 + i).wait()

        @pl.when(level >= 5)
        def _():
            from_late(level + 7).wait()

        for c in range(CAP):
            r = rows[c]
            total = None
            for k in range(0, 4 * SLOTS, 2):
                pieces = [table[lookup[c * 4 * SLOTS + k + i]] for i in range(2)]
                factors = [blocks[places[c], lax.rem(z + (k + i) // SLOTS, 4), (k + i) % SLOTS] for i in range(2)]
                term = dot_t(jnp.concatenate(pieces, axis=1), jnp.concatenate(factors, axis=1))
                total = term if total is None else total + term
            v = times_inverse(rhs[r] - total, inv_terms[r])
            sol[level * CAP + c] = v
            land[p_next, q, x, y, c] = v.astype(jnp.bfloat16)

        @pl.when(level < LEV - 1)
        def _():
            start_spread(p_next)

        return carry

    lax.fori_loop(1, LEV, body, 0)

    for t in range(SENT):
        for copy in direct(t) + [forward(t)]:
            copy.wait_send()
    give(range(ROWS - CAP, ROWS))


def per_device(factor_blocks, pattern, levels, diag_inverse, right_side):
    bf, f32, dma = jnp.bfloat16, jnp.float32, pltpu.SemaphoreType.DMA
    vmem = pltpu.VMEM
    out = pl.pallas_call(
        kernel,
        out_shape=pltpu.VMEM((ROWS, W, B), f32),
        in_specs=[
            pl.BlockSpec(memory_space=pl.ANY),
            pl.BlockSpec(memory_space=pltpu.SMEM),
            pl.BlockSpec(memory_space=pltpu.SMEM),
            pl.BlockSpec(memory_space=pl.ANY),
            pl.BlockSpec(memory_space=pl.ANY),
        ],
        out_specs=pl.BlockSpec(memory_space=pltpu.VMEM),
        scratch_shapes=[
            vmem((ROWS, SLOTS, B, B), bf),
            vmem((SENT, 4, SLOTS, B, B), bf),
            vmem((SENT - EARLY, 4, SLOTS, B, B), bf),
            vmem((CAP, B, B), f32),
            vmem((ROWS, B, B), f32),
            vmem((ROWS, 2 * B, B), bf),
            vmem((ROWS, W, B), f32),
            pltpu.SMEM((3, SLOTS, ROWS), jnp.int32),
            vmem((EMPTY + 1, W, B), bf),
            vmem((2, 2, 4, 4, CAP, W, B), bf),
            vmem((LEV * CAP, W, B), f32),
            pltpu.SMEM((CAP * 4 * SLOTS,), jnp.int32),
            pltpu.SMEM((CAP,), jnp.int32),
            pltpu.SMEM((CAP,), jnp.int32),
            dma((5,)), dma((SENT - EARLY,)), dma((3,)), dma((3,)),
            dma((SENT, 3)), dma((SENT, 3)),
            dma((2, 4, 4)), dma((2, 4, 4)), dma((2, 4)), dma((2, 4)),
        ],
        compiler_params=pltpu.CompilerParams(
            collective_id=0, has_side_effects=True, vmem_limit_bytes=56 * 1024 * 1024
        ),
    )(factor_blocks, pattern.T, levels, diag_inverse, jnp.swapaxes(right_side, 1, 2))
    return jnp.swapaxes(out, 1, 2)


def solution(mesh):
    return jax.shard_map(
        per_device,
        mesh=mesh,
        in_specs=(
            P("row", "col", None, None),
            P("row", "col"),
            P(),
            P("row", None, None),
            P("row", None, "col"),
        ),
        out_specs=P("row", None, "col"),
        check_vma=False,
    )
```

```python
import jax
import jax.numpy as jnp
from jax import lax
from jax.experimental import pallas as pl
from jax.experimental.pallas import tpu as pltpu
from jax.sharding import PartitionSpec as P

MESH = pl.DeviceIdType.MESH
LEV = 8
CAP = 3
B = 128
W = 32
ROWS = 16
SLOTS = 5
EMPTY = (LEV - 1) * 32 * CAP
SENT = ROWS - 1
EARLY = 3
AHEAD = 2


def dot_t(a, b):
    return lax.dot_general(a, b, (((1,), (1,)), ((), ())), preferred_element_type=jnp.float32)


def split(a):
    high = a.astype(jnp.bfloat16)
    return high, (a - high.astype(jnp.float32)).astype(jnp.bfloat16)


def both_terms(d):
    return jnp.concatenate(split(d), axis=0)


def times_inverse(v, d):
    n = v.shape[0]
    v_high, v_low = split(v)
    terms = dot_t(jnp.concatenate([v_high, v_low], axis=0), d)
    return terms[:n, :B] + (terms[n:, :B] + terms[:n, B:])


def kernel(
    factor, pattern, levels, inverse, right, out,
    raw, blocks, late, inv0, inv, inv_terms, rhs, pats, table, land, sol, lookup, rows, places,
    local_sem, late_sem, pat_s, pat_r, zs, zr, gs, gr, cs, cr,
):
    row, z = lax.axis_index("row"), lax.axis_index("col")
    x, y, q = row // 8, lax.rem(row // 2, 4), lax.rem(row, 2)
    chip = x * 4 + y
    partner = (chip * 2 + 1 - q, z)

    def along_z(by):
        return (row, lax.rem(z + by, 4))

    def remote(src, dst, s, r, to):
        return pltpu.make_async_remote_copy(
            src_ref=src, dst_ref=dst, send_sem=s, recv_sem=r, device_id=to, device_id_type=MESH
        )

    own = [
        pltpu.make_async_copy(inverse.at[0:CAP], inv0, local_sem.at[0]),
        pltpu.make_async_copy(inverse, inv, local_sem.at[1]),
        pltpu.make_async_copy(factor, raw, local_sem.at[2]),
        pltpu.make_async_copy(right.at[0:CAP], rhs.at[0:CAP], local_sem.at[3]),
        pltpu.make_async_copy(right.at[CAP:ROWS], rhs.at[CAP:ROWS], local_sem.at[4]),
    ]

    offsets = [(dx, dy) for dx in range(4) for dy in range(4) if (dx, dy) != (0, 0)]
    offsets.sort(key=lambda o: -(min(o[0], 4 - o[0]) + min(o[1], 4 - o[1])))

    def in_plane(dx, dy):
        return ((lax.rem(x + dx, 4) * 4 + lax.rem(y + dy, 4)) * 2 + q, z)

    barrier = pltpu.get_barrier_semaphore()
    greeted = [partner] + [along_z(by) for by in (1, 2, 3)] + [in_plane(*o) for o in offsets]
    for to in greeted:
        pl.semaphore_signal(barrier, inc=1, device_id=to, device_id_type=MESH)
    for i in (2, 0, 3, 1, 4):
        own[i].start()
    table[EMPTY] = jnp.zeros(table.shape[1:], table.dtype)

    def count_below(level):
        count = jnp.int32(0)
        for r in range(ROWS):
            count += (levels[row * ROWS + r] < level).astype(jnp.int32)
        return count

    skipped = count_below(1)
    own[2].wait()
    for n in range(EARLY):
        blocks[n, z] = raw[jnp.minimum(skipped + n, ROWS - 1)]

    def shift(n, carry):
        late[n - EARLY, z] = raw[jnp.minimum(skipped + n, ROWS - 1)]
        return carry

    lax.fori_loop(EARLY, SENT, shift, 0)
    pl.semaphore_wait(barrier, len(greeted))

    def home(t, owner):
        if isinstance(t, int) and t < EARLY:
            return blocks.at[t, owner]
        return late.at[t - EARLY, owner]

    def direct(t):
        return [remote(home(t, z), home(t, z), zs.at[t, k], zr.at[t, k], along_z(1 + 2 * k)) for k in range(2)]

    def arrives(t, k, owner):
        unit = home(t, owner)
        return remote(unit, unit, zs.at[t, k], zr.at[t, k], along_z(1))

    def forward(t):
        by = 1 + 2 * lax.rem(t + q, 2)
        unit = home(t, lax.rem(z + 4 - by, 4))
        return remote(unit, unit, zs.at[t, 2], zr.at[t, 2], along_z(by))

    def pass_on(t):
        k = lax.rem(t + q, 2)
        arrives(t, k, lax.rem(z + 3 - 2 * k, 4)).wait_recv()
        forward(t).start()

    def send_ahead(t):
        for copy in direct(t):
            copy.start()

    def arrive(t):
        k = lax.rem(t + q, 2)
        arrives(t, 1 - k, lax.rem(z + 1 + 2 * k, 4)).wait_recv()
        arrives(t, 2, lax.rem(z + 2, 4)).wait_recv()

    def pattern_copies():
        return [remote(pattern, pats.at[3 - by], pat_s.at[by - 1], pat_r.at[by - 1], along_z(by)) for by in (1, 2, 3)]

    def pattern_arrives():
        return [remote(pats.at[3 - by], pats.at[3 - by], pat_s.at[by - 1], pat_r.at[by - 1], along_z(by)) for by in (1, 2, 3)]

    for copy in pattern_copies():
        copy.start()
    for t in range(AHEAD):
        send_ahead(t)

    def spread(p, dx, dy):
        unit = land.at[p, q, x, y]
        return remote(unit, unit, gs.at[p, dx, dy], gr.at[p, dx, dy], in_plane(dx, dy))

    def spread_in(p, dx, dy):
        unit = land.at[p, q, lax.rem(x + 4 - dx, 4), lax.rem(y + 4 - dy, 4)]
        return remote(unit, unit, gs.at[p, dx, dy], gr.at[p, dx, dy], in_plane(dx, dy))

    def across(p, dx, core):
        unit = land.at[p, core, lax.rem(x + 4 - dx, 4)]
        return remote(unit, unit, cs.at[p, dx], cr.at[p, dx], partner)

    def start_spread(p):
        for o in offsets:
            spread(p, *o).start()

    own[0].wait()
    own[3].wait()
    for c in range(CAP):
        v = times_inverse(rhs[c], both_terms(inv0[c]))
        sol[c] = v
        land[0, q, x, y, c] = v.astype(jnp.bfloat16)
    start_spread(0)
    own[1].wait()
    own[4].wait()

    def prepare(r, carry):
        inv_terms[r] = both_terms(inv[r])
        return carry

    lax.fori_loop(0, ROWS, prepare, 0)

    def find(level):
        start = count_below(level)
        for c in range(CAP):
            r = jnp.minimum(start + c, ROWS - 1)
            rows[c] = r
            places[c] = jnp.clip(r - skipped, 0, SENT - 1)
            for k in range(4 * SLOTS):
                far, slot = k // SLOTS, k % SLOTS
                j = pattern[slot, r] if far == 0 else pats[far - 1, slot, r]
                j0 = jnp.maximum(j, 0)
                inside = lax.rem(j0, ROWS)
                its = levels[j0]
                rank = ((levels[jnp.maximum(j0 - 1, 0)] == its) & (inside >= 1)).astype(jnp.int32) + (
                    (levels[jnp.maximum(j0 - 2, 0)] == its) & (inside >= 2)
                ).astype(jnp.int32)
                group = j0 // ROWS
                at = ((its * 2 + lax.rem(group, 2)) * 16 + group // 2) * CAP + rank
                lookup[c * 4 * SLOTS + k] = jnp.where(j < 0, EMPTY, jnp.minimum(at, EMPTY))

    def from_late(t):
        return pltpu.make_async_copy(late.at[t - EARLY], blocks.at[t], late_sem.at[t - EARLY])

    def sent(p):
        for o in offsets:
            spread(p, *o).wait_send()

    def give(some):
        for r in some:
            its = levels[row * ROWS + r]
            rank = jnp.int32(0)
            for back in (1, 2):
                if r >= back:
                    rank += (levels[row * ROWS + r - back] == its).astype(jnp.int32)
            out[r] = sol[its * CAP + rank]

    def body(level, carry):
        p = lax.rem(level - 1, 2)
        p_next = lax.rem(level, 2)

        @pl.when(level == 1)
        def _():
            pass_on(0)
            send_ahead(AHEAD)
            for copy in pattern_arrives():
                copy.wait_recv()
            for copy in pattern_copies():
                copy.wait_send()

        find(level)

        @pl.when(level >= 2)
        def _():
            sent(p_next)

        @pl.when(level == LEV - 1)
        def _():
            give(range(ROWS - CAP))

        @pl.when((level >= 2) & (level <= 4))
        def _():
            pass_on(3 * level - 3)

        @pl.when((level == 5) | (level == 6))
        def _():
            pass_on(2 * level + 2)

        for dx in (0, 1, 3, 2):
            for dy in (1, 3, 2, 0):
                if (dx, dy) != (0, 0):
                    spread_in(p, dx, dy).wait_recv()
            across(p, dx, q).start()

        @pl.when(level == 1)
        def _():
            for t in range(1, EARLY):
                pass_on(t)
            send_ahead(EARLY)
            send_ahead(EARLY + 1)
            for t in range(EARLY):
                arrive(t)
            send_ahead(EARLY + 2)

        @pl.when((level >= 2) & (level <= 4))
        def _():
            for i in (1, 2):
                pass_on(3 * level - 3 + i)
            send_ahead(3 * level)
            for i in range(3):
                arrive(3 * level - 3 + i)
                from_late(3 * level - 3 + i).start()
            send_ahead(3 * level + 1)
            send_ahead(3 * level + 2)

        @pl.when(level == 5)
        def _():
            pass_on(jnp.int32(13))

        @pl.when(level >= 5)
        def _():
            arrive(level + 7)
            from_late(level + 7).start()

        for dx in range(4):
            across(p, dx, q).wait_send()
            across(p, dx, 1 - q).wait_recv()

        def to_table(i, carry):
            a, b = i // 4, lax.rem(i, 4)
            for core in range(2):
                for c in range(CAP):
                    table[(((level - 1) * 2 + core) * 16 + i) * CAP + c] = land[p, core, a, b, c]
            return carry

        lax.fori_loop(0, 16, to_table, 0, unroll=4)

        @pl.when((level >= 2) & (level <= 4))
        def _():
            for i in range(3):
                from_late(3 * level - 3 + i).wait()

        @pl.when(level >= 5)
        def _():
            from_late(level + 7).wait()

        for c in range(CAP):
            r = rows[c]
            total = None
            for k in range(0, 4 * SLOTS, 4):
                pieces = [table[lookup[c * 4 * SLOTS + k + i]] for i in range(4)]
                factors = [blocks[places[c], lax.rem(z + (k + i) // SLOTS, 4), (k + i) % SLOTS] for i in range(4)]
                term = dot_t(jnp.concatenate(pieces, axis=1), jnp.concatenate(factors, axis=1))
                total = term if total is None else total + term
            v = times_inverse(rhs[r] - total, inv_terms[r])
            sol[level * CAP + c] = v
            land[p_next, q, x, y, c] = v.astype(jnp.bfloat16)

        @pl.when(level < LEV - 1)
        def _():
            start_spread(p_next)

        return carry

    lax.fori_loop(1, LEV, body, 0)
    sent((LEV - 2) % 2)

    for t in range(SENT):
        for copy in direct(t) + [forward(t)]:
            copy.wait_send()
    give(range(ROWS - CAP, ROWS))


def per_device(factor_blocks, pattern, levels, diag_inverse, right_side):
    bf, f32, dma = jnp.bfloat16, jnp.float32, pltpu.SemaphoreType.DMA
    vmem = pltpu.VMEM
    out = pl.pallas_call(
        kernel,
        out_shape=pltpu.VMEM((ROWS, W, B), f32),
        in_specs=[
            pl.BlockSpec(memory_space=pl.ANY),
            pl.BlockSpec(memory_space=pltpu.SMEM),
            pl.BlockSpec(memory_space=pltpu.SMEM),
            pl.BlockSpec(memory_space=pl.ANY),
            pl.BlockSpec(memory_space=pl.ANY),
        ],
        out_specs=pl.BlockSpec(memory_space=pltpu.VMEM),
        scratch_shapes=[
            vmem((ROWS, SLOTS, B, B), bf),
            vmem((SENT, 4, SLOTS, B, B), bf),
            vmem((SENT - EARLY, 4, SLOTS, B, B), bf),
            vmem((CAP, B, B), f32),
            vmem((ROWS, B, B), f32),
            vmem((ROWS, 2 * B, B), bf),
            vmem((ROWS, W, B), f32),
            pltpu.SMEM((3, SLOTS, ROWS), jnp.int32),
            vmem((EMPTY + 1, W, B), bf),
            vmem((2, 2, 4, 4, CAP, W, B), bf),
            vmem((LEV * CAP, W, B), f32),
            pltpu.SMEM((CAP * 4 * SLOTS,), jnp.int32),
            pltpu.SMEM((CAP,), jnp.int32),
            pltpu.SMEM((CAP,), jnp.int32),
            dma((5,)), dma((SENT - EARLY,)), dma((3,)), dma((3,)),
            dma((SENT, 3)), dma((SENT, 3)),
            dma((2, 4, 4)), dma((2, 4, 4)), dma((2, 4)), dma((2, 4)),
        ],
        compiler_params=pltpu.CompilerParams(
            collective_id=0, has_side_effects=True, vmem_limit_bytes=56 * 1024 * 1024
        ),
    )(factor_blocks, pattern.T, levels, diag_inverse, jnp.swapaxes(right_side, 1, 2))
    return jnp.swapaxes(out, 1, 2)


def solution(mesh):
    return jax.shard_map(
        per_device,
        mesh=mesh,
        in_specs=(
            P("row", "col", None, None),
            P("row", "col"),
            P(),
            P("row", None, None),
            P("row", None, "col"),
        ),
        out_specs=P("row", None, "col"),
        check_vma=False,
    )
```

```python
import jax
import jax.numpy as jnp
from jax import lax
from jax.experimental import pallas as pl
from jax.experimental.pallas import tpu as pltpu
from jax.sharding import PartitionSpec as P

MESH = pl.DeviceIdType.MESH
LEV = 8
CAP = 3
B = 128
W = 32
ROWS = 16
SLOTS = 5
EMPTY = (LEV - 1) * 32 * CAP
SENT = ROWS - 1
EARLY = 3
AHEAD = 2


def dot_t(a, b):
    return lax.dot_general(a, b, (((1,), (1,)), ((), ())), preferred_element_type=jnp.float32)


def split(a):
    high = a.astype(jnp.bfloat16)
    return high, (a - high.astype(jnp.float32)).astype(jnp.bfloat16)


def both_terms(d):
    return jnp.concatenate(split(d), axis=0)


def times_inverse(v, d):
    n = v.shape[0]
    v_high, v_low = split(v)
    terms = dot_t(jnp.concatenate([v_high, v_low], axis=0), d)
    return terms[:n, :B] + (terms[n:, :B] + terms[:n, B:])


def kernel(
    factor, pattern, levels, inverse, right, out,
    raw, blocks, late, inv0, inv, inv_terms, rhs, pats, table, land, sol, lookup, rows, places,
    local_sem, late_sem, pat_s, pat_r, zs, zr, gs, gr, cs, cr,
):
    row, z = lax.axis_index("row"), lax.axis_index("col")
    x, y, q = row // 8, lax.rem(row // 2, 4), lax.rem(row, 2)
    chip = x * 4 + y
    partner = (chip * 2 + 1 - q, z)

    def along_z(by):
        return (row, lax.rem(z + by, 4))

    def remote(src, dst, s, r, to):
        return pltpu.make_async_remote_copy(
            src_ref=src, dst_ref=dst, send_sem=s, recv_sem=r, device_id=to, device_id_type=MESH
        )

    own = [
        pltpu.make_async_copy(inverse.at[0:CAP], inv0, local_sem.at[0]),
        pltpu.make_async_copy(inverse, inv, local_sem.at[1]),
        pltpu.make_async_copy(factor, raw, local_sem.at[2]),
        pltpu.make_async_copy(right.at[0:CAP], rhs.at[0:CAP], local_sem.at[3]),
        pltpu.make_async_copy(right.at[CAP:ROWS], rhs.at[CAP:ROWS], local_sem.at[4]),
    ]

    offsets = [(dx, dy) for dx in range(4) for dy in range(4) if (dx, dy) != (0, 0)]
    offsets.sort(key=lambda o: -(min(o[0], 4 - o[0]) + min(o[1], 4 - o[1])))

    def in_plane(dx, dy):
        return ((lax.rem(x + dx, 4) * 4 + lax.rem(y + dy, 4)) * 2 + q, z)

    barrier = pltpu.get_barrier_semaphore()
    greeted = [partner] + [along_z(by) for by in (1, 2, 3)] + [in_plane(*o) for o in offsets]
    for to in greeted:
        pl.semaphore_signal(barrier, inc=1, device_id=to, device_id_type=MESH)
    for i in (2, 0, 3, 1, 4):
        own[i].start()
    table[EMPTY] = jnp.zeros(table.shape[1:], table.dtype)

    def count_below(level):
        count = jnp.int32(0)
        for r in range(ROWS):
            count += (levels[row * ROWS + r] < level).astype(jnp.int32)
        return count

    skipped = count_below(1)
    own[2].wait()
    for n in range(EARLY):
        blocks[n, z] = raw[jnp.minimum(skipped + n, ROWS - 1)]

    def shift(n, carry):
        late[n - EARLY, z] = raw[jnp.minimum(skipped + n, ROWS - 1)]
        return carry

    lax.fori_loop(EARLY, SENT, shift, 0)
    pl.semaphore_wait(barrier, len(greeted))

    def home(t, owner):
        if isinstance(t, int) and t < EARLY:
            return blocks.at[t, owner]
        return late.at[t - EARLY, owner]

    def direct(t):
        return [remote(home(t, z), home(t, z), zs.at[t, k], zr.at[t, k], along_z(1 + 2 * k)) for k in range(2)]

    def arrives(t, k, owner):
        unit = home(t, owner)
        return remote(unit, unit, zs.at[t, k], zr.at[t, k], along_z(1))

    def forward(t):
        by = 1 + 2 * lax.rem(t + q, 2)
        unit = home(t, lax.rem(z + 4 - by, 4))
        return remote(unit, unit, zs.at[t, 2], zr.at[t, 2], along_z(by))

    def pass_on(t):
        k = lax.rem(t + q, 2)
        arrives(t, k, lax.rem(z + 3 - 2 * k, 4)).wait_recv()
        forward(t).start()

    def send_ahead(t):
        for copy in direct(t):
            copy.start()

    def arrive(t):
        k = lax.rem(t + q, 2)
        arrives(t, 1 - k, lax.rem(z + 1 + 2 * k, 4)).wait_recv()
        arrives(t, 2, lax.rem(z + 2, 4)).wait_recv()

    def pattern_copies():
        return [remote(pattern, pats.at[3 - by], pat_s.at[by - 1], pat_r.at[by - 1], along_z(by)) for by in (1, 2, 3)]

    def pattern_arrives():
        return [remote(pats.at[3 - by], pats.at[3 - by], pat_s.at[by - 1], pat_r.at[by - 1], along_z(by)) for by in (1, 2, 3)]

    for copy in pattern_copies():
        copy.start()
    for t in range(AHEAD):
        send_ahead(t)

    def spread(p, dx, dy):
        unit = land.at[p, q, x, y]
        return remote(unit, unit, gs.at[p, dx], gr.at[p, dx], in_plane(dx, dy))

    def spread_group(p, dx):
        unit = land.at[p, q, lax.rem(x + 4 - dx, 4), pl.ds(0, 4 if dx else 3)]
        return remote(unit, unit, gs.at[p, dx], gr.at[p, dx], partner)

    def across(p, dx, core):
        unit = land.at[p, core, lax.rem(x + 4 - dx, 4)]
        return remote(unit, unit, cs.at[p, dx], cr.at[p, dx], partner)

    def start_spread(p):
        for o in offsets:
            spread(p, *o).start()

    own[0].wait()
    own[3].wait()
    for c in range(CAP):
        v = times_inverse(rhs[c], both_terms(inv0[c]))
        sol[c] = v
        land[0, q, x, y, c] = v.astype(jnp.bfloat16)
    start_spread(0)
    own[1].wait()
    own[4].wait()

    def prepare(r, carry):
        inv_terms[r] = both_terms(inv[r])
        return carry

    lax.fori_loop(0, ROWS, prepare, 0)

    def find(level):
        start = count_below(level)
        for c in range(CAP):
            r = jnp.minimum(start + c, ROWS - 1)
            rows[c] = r
            places[c] = jnp.clip(r - skipped, 0, SENT - 1)
            for k in range(4 * SLOTS):
                far, slot = k // SLOTS, k % SLOTS
                j = pattern[slot, r] if far == 0 else pats[far - 1, slot, r]
                j0 = jnp.maximum(j, 0)
                inside = lax.rem(j0, ROWS)
                its = levels[j0]
                rank = ((levels[jnp.maximum(j0 - 1, 0)] == its) & (inside >= 1)).astype(jnp.int32) + (
                    (levels[jnp.maximum(j0 - 2, 0)] == its) & (inside >= 2)
                ).astype(jnp.int32)
                group = j0 // ROWS
                at = ((its * 2 + lax.rem(group, 2)) * 16 + group // 2) * CAP + rank
                lookup[c * 4 * SLOTS + k] = jnp.where(j < 0, EMPTY, jnp.minimum(at, EMPTY))

    def from_late(t):
        return pltpu.make_async_copy(late.at[t - EARLY], blocks.at[t], late_sem.at[t - EARLY])

    def sent(p):
        for dx in range(4):
            spread_group(p, dx).wait_send()

    def give(some):
        for r in some:
            its = levels[row * ROWS + r]
            rank = jnp.int32(0)
            for back in (1, 2):
                if r >= back:
                    rank += (levels[row * ROWS + r - back] == its).astype(jnp.int32)
            out[r] = sol[its * CAP + rank]

    def body(level, carry):
        p = lax.rem(level - 1, 2)
        p_next = lax.rem(level, 2)

        @pl.when(level == 1)
        def _():
            pass_on(0)
            send_ahead(AHEAD)
            for copy in pattern_arrives():
                copy.wait_recv()
            for copy in pattern_copies():
                copy.wait_send()

        find(level)

        @pl.when(level >= 2)
        def _():
            sent(p_next)

        @pl.when(level == LEV - 1)
        def _():
            give(range(ROWS - CAP))

        @pl.when((level >= 2) & (level <= 4))
        def _():
            pass_on(3 * level - 3)

        @pl.when((level == 5) | (level == 6))
        def _():
            pass_on(2 * level + 2)

        for dx in (0, 1, 3, 2):
            spread_group(p, dx).wait_recv()
            across(p, dx, q).start()

        @pl.when(level == 1)
        def _():
            for t in range(1, EARLY):
                pass_on(t)
            send_ahead(EARLY)
            send_ahead(EARLY + 1)
            for t in range(EARLY):
                arrive(t)
            send_ahead(EARLY + 2)

        @pl.when((level >= 2) & (level <= 4))
        def _():
            for i in (1, 2):
                pass_on(3 * level - 3 + i)
            send_ahead(3 * level)
            for i in range(3):
                arrive(3 * level - 3 + i)
                from_late(3 * level - 3 + i).start()
            send_ahead(3 * level + 1)
            send_ahead(3 * level + 2)

        @pl.when(level == 5)
        def _():
            pass_on(jnp.int32(13))

        @pl.when(level >= 5)
        def _():
            arrive(level + 7)
            from_late(level + 7).start()

        for dx in range(4):
            across(p, dx, 1 - q).wait_recv()

        def to_table(i, carry):
            a, b = i // 4, lax.rem(i, 4)
            for core in range(2):
                for c in range(CAP):
                    table[(((level - 1) * 2 + core) * 16 + i) * CAP + c] = land[p, core, a, b, c]
            return carry

        lax.fori_loop(0, 16, to_table, 0, unroll=4)

        @pl.when((level >= 2) & (level <= 4))
        def _():
            for i in range(3):
                from_late(3 * level - 3 + i).wait()

        @pl.when(level >= 5)
        def _():
            from_late(level + 7).wait()

        for c in range(CAP):
            r = rows[c]
            total = None
            for k in range(0, 4 * SLOTS, 20):
                pieces = [table[lookup[c * 4 * SLOTS + k + i]] for i in range(20)]
                factors = [blocks[places[c], lax.rem(z + (k + i) // SLOTS, 4), (k + i) % SLOTS] for i in range(20)]
                term = dot_t(jnp.concatenate(pieces, axis=1), jnp.concatenate(factors, axis=1))
                total = term if total is None else total + term
            v = times_inverse(rhs[r] - total, inv_terms[r])
            sol[level * CAP + c] = v
            land[p_next, q, x, y, c] = v.astype(jnp.bfloat16)

        for dx in range(4):
            across(p, dx, q).wait_send()

        @pl.when(level < LEV - 1)
        def _():
            start_spread(p_next)

        return carry

    lax.fori_loop(1, LEV, body, 0)
    sent((LEV - 2) % 2)

    for t in range(SENT):
        for copy in direct(t) + [forward(t)]:
            copy.wait_send()
    give(range(ROWS - CAP, ROWS))


def per_device(factor_blocks, pattern, levels, diag_inverse, right_side):
    bf, f32, dma = jnp.bfloat16, jnp.float32, pltpu.SemaphoreType.DMA
    vmem = pltpu.VMEM
    out = pl.pallas_call(
        kernel,
        out_shape=pltpu.VMEM((ROWS, W, B), f32),
        in_specs=[
            pl.BlockSpec(memory_space=pl.ANY),
            pl.BlockSpec(memory_space=pltpu.SMEM),
            pl.BlockSpec(memory_space=pltpu.SMEM),
            pl.BlockSpec(memory_space=pl.ANY),
            pl.BlockSpec(memory_space=pl.ANY),
        ],
        out_specs=pl.BlockSpec(memory_space=pltpu.VMEM),
        scratch_shapes=[
            vmem((ROWS, SLOTS, B, B), bf),
            vmem((SENT, 4, SLOTS, B, B), bf),
            vmem((SENT - EARLY, 4, SLOTS, B, B), bf),
            vmem((CAP, B, B), f32),
            vmem((ROWS, B, B), f32),
            vmem((ROWS, 2 * B, B), bf),
            vmem((ROWS, W, B), f32),
            pltpu.SMEM((3, SLOTS, ROWS), jnp.int32),
            vmem((EMPTY + 1, W, B), bf),
            vmem((2, 2, 4, 4, CAP, W, B), bf),
            vmem((LEV * CAP, W, B), f32),
            pltpu.SMEM((CAP * 4 * SLOTS,), jnp.int32),
            pltpu.SMEM((CAP,), jnp.int32),
            pltpu.SMEM((CAP,), jnp.int32),
            dma((5,)), dma((SENT - EARLY,)), dma((3,)), dma((3,)),
            dma((SENT, 3)), dma((SENT, 3)),
            dma((2, 4)), dma((2, 4)), dma((2, 4)), dma((2, 4)),
        ],
        compiler_params=pltpu.CompilerParams(
            collective_id=0, has_side_effects=True, vmem_limit_bytes=56 * 1024 * 1024
        ),
    )(factor_blocks, pattern.T, levels, diag_inverse, jnp.swapaxes(right_side, 1, 2))
    return jnp.swapaxes(out, 1, 2)


def solution(mesh):
    return jax.shard_map(
        per_device,
        mesh=mesh,
        in_specs=(
            P("row", "col", None, None),
            P("row", "col"),
            P(),
            P("row", None, None),
            P("row", None, "col"),
        ),
        out_specs=P("row", None, "col"),
        check_vma=False,
    )
```

```python
import jax
import jax.numpy as jnp
from jax import lax
from jax.experimental import pallas as pl
from jax.experimental.pallas import tpu as pltpu
from jax.sharding import PartitionSpec as P

MESH = pl.DeviceIdType.MESH
LEV = 8
CAP = 3
B = 128
W = 32
ROWS = 16
SLOTS = 5
EMPTY = (LEV - 1) * 32 * CAP
SENT = ROWS - 1
EARLY = 3
AHEAD = 2


def dot_t(a, b):
    return lax.dot_general(a, b, (((1,), (1,)), ((), ())), preferred_element_type=jnp.float32)


def split(a):
    high = a.astype(jnp.bfloat16)
    return high, (a - high.astype(jnp.float32)).astype(jnp.bfloat16)


def both_terms(d):
    return jnp.concatenate(split(d), axis=0)


def times_inverse(v, d):
    n = v.shape[0]
    v_high, v_low = split(v)
    terms = dot_t(jnp.concatenate([v_high, v_low], axis=0), d)
    return terms[:n, :B] + (terms[n:, :B] + terms[:n, B:])


def kernel(
    factor, pattern, levels, inverse, right, out,
    raw, blocks, late, inv0, inv, inv_terms, rhs, pats, table, land, sol, lookup, rows, places,
    local_sem, late_sem, pat_s, pat_r, zs, zr, gs, gr, cs, cr,
):
    row, z = lax.axis_index("row"), lax.axis_index("col")
    x, y, q = row // 8, lax.rem(row // 2, 4), lax.rem(row, 2)
    chip = x * 4 + y
    partner = (chip * 2 + 1 - q, z)

    def along_z(by):
        return (row, lax.rem(z + by, 4))

    def remote(src, dst, s, r, to):
        return pltpu.make_async_remote_copy(
            src_ref=src, dst_ref=dst, send_sem=s, recv_sem=r, device_id=to, device_id_type=MESH
        )

    own = [
        pltpu.make_async_copy(inverse.at[0:CAP], inv0, local_sem.at[0]),
        pltpu.make_async_copy(inverse, inv, local_sem.at[1]),
        pltpu.make_async_copy(factor, raw, local_sem.at[2]),
        pltpu.make_async_copy(right.at[0:CAP], rhs.at[0:CAP], local_sem.at[3]),
        pltpu.make_async_copy(right.at[CAP:ROWS], rhs.at[CAP:ROWS], local_sem.at[4]),
    ]

    offsets = [(dx, dy) for dx in range(4) for dy in range(4) if (dx, dy) != (0, 0)]
    offsets.sort(key=lambda o: -(min(o[0], 4 - o[0]) + min(o[1], 4 - o[1])))

    def in_plane(dx, dy):
        return ((lax.rem(x + dx, 4) * 4 + lax.rem(y + dy, 4)) * 2 + q, z)

    barrier = pltpu.get_barrier_semaphore()
    greeted = [partner] + [along_z(by) for by in (1, 2, 3)] + [in_plane(*o) for o in offsets]
    for to in greeted:
        pl.semaphore_signal(barrier, inc=1, device_id=to, device_id_type=MESH)
    for i in (2, 0, 3, 1, 4):
        own[i].start()
    table[EMPTY] = jnp.zeros(table.shape[1:], table.dtype)

    def count_below(level):
        count = jnp.int32(0)
        for r in range(ROWS):
            count += (levels[row * ROWS + r] < level).astype(jnp.int32)
        return count

    skipped = count_below(1)
    own[2].wait()
    for n in range(EARLY):
        blocks[n, z] = raw[jnp.minimum(skipped + n, ROWS - 1)]

    def shift(n, carry):
        late[n - EARLY, z] = raw[jnp.minimum(skipped + n, ROWS - 1)]
        return carry

    lax.fori_loop(EARLY, SENT, shift, 0)
    pl.semaphore_wait(barrier, len(greeted))

    def home(t, owner):
        if isinstance(t, int) and t < EARLY:
            return blocks.at[t, owner]
        return late.at[t - EARLY, owner]

    def direct(t):
        return [remote(home(t, z), home(t, z), zs.at[t, k], zr.at[t, k], along_z(1 + 2 * k)) for k in range(2)]

    def arrives(t, k, owner):
        unit = home(t, owner)
        return remote(unit, unit, zs.at[t, k], zr.at[t, k], along_z(1))

    def forward(t):
        by = 1 + 2 * lax.rem(t + q, 2)
        unit = home(t, lax.rem(z + 4 - by, 4))
        return remote(unit, unit, zs.at[t, 2], zr.at[t, 2], along_z(by))

    def pass_on(t):
        k = lax.rem(t + q, 2)
        arrives(t, k, lax.rem(z + 3 - 2 * k, 4)).wait_recv()
        forward(t).start()

    def send_ahead(t):
        for copy in direct(t):
            copy.start()

    def arrive(t):
        k = lax.rem(t + q, 2)
        arrives(t, 1 - k, lax.rem(z + 1 + 2 * k, 4)).wait_recv()
        arrives(t, 2, lax.rem(z + 2, 4)).wait_recv()

    def pattern_copies():
        return [remote(pattern, pats.at[3 - by], pat_s.at[by - 1], pat_r.at[by - 1], along_z(by)) for by in (1, 2, 3)]

    def pattern_arrives():
        return [remote(pats.at[3 - by], pats.at[3 - by], pat_s.at[by - 1], pat_r.at[by - 1], along_z(by)) for by in (1, 2, 3)]

    for copy in pattern_copies():
        copy.start()
    for t in range(AHEAD):
        send_ahead(t)

    def spread(p, dx, dy):
        unit = land.at[p, q, x, y]
        return remote(unit, unit, gs.at[p, dx], gr.at[p, dx], in_plane(dx, dy))

    def spread_group(p, dx):
        unit = land.at[p, q, lax.rem(x + 4 - dx, 4), pl.ds(0, 4 if dx else 3)]
        return remote(unit, unit, gs.at[p, dx], gr.at[p, dx], partner)

    def across(p, dx, core):
        unit = land.at[p, core, lax.rem(x + 4 - dx, 4)]
        return remote(unit, unit, cs.at[p, dx], cr.at[p, dx], partner)

    def start_spread(p):
        for o in offsets:
            spread(p, *o).start()

    own[0].wait()
    own[3].wait()
    for c in range(CAP):
        v = times_inverse(rhs[c], both_terms(inv0[c]))
        sol[c] = v
        land[0, q, x, y, c] = v.astype(jnp.bfloat16)
    start_spread(0)
    own[1].wait()
    own[4].wait()

    def prepare(r, carry):
        inv_terms[r] = both_terms(inv[r])
        return carry

    lax.fori_loop(0, ROWS, prepare, 0)

    def find(level):
        start = count_below(level)
        for c in range(CAP):
            r = jnp.minimum(start + c, ROWS - 1)
            rows[c] = r
            places[c] = jnp.clip(r - skipped, 0, SENT - 1)
            for k in range(4 * SLOTS):
                far, slot = k // SLOTS, k % SLOTS
                j = pattern[slot, r] if far == 0 else pats[far - 1, slot, r]
                j0 = jnp.maximum(j, 0)
                inside = lax.rem(j0, ROWS)
                its = levels[j0]
                rank = ((levels[jnp.maximum(j0 - 1, 0)] == its) & (inside >= 1)).astype(jnp.int32) + (
                    (levels[jnp.maximum(j0 - 2, 0)] == its) & (inside >= 2)
                ).astype(jnp.int32)
                group = j0 // ROWS
                at = ((its * 2 + lax.rem(group, 2)) * 16 + group // 2) * CAP + rank
                lookup[c * 4 * SLOTS + k] = jnp.where(j < 0, EMPTY, jnp.minimum(at, EMPTY))

    def from_late(t):
        return pltpu.make_async_copy(late.at[t - EARLY], blocks.at[t], late_sem.at[t - EARLY])

    def sent(p):
        for dx in range(4):
            spread_group(p, dx).wait_send()

    def give(some):
        for r in some:
            its = levels[row * ROWS + r]
            rank = jnp.int32(0)
            for back in (1, 2):
                if r >= back:
                    rank += (levels[row * ROWS + r - back] == its).astype(jnp.int32)
            out[r] = sol[its * CAP + rank]

    def body(level, carry):
        p = lax.rem(level - 1, 2)
        p_next = lax.rem(level, 2)

        @pl.when(level == 1)
        def _():
            pass_on(0)
            send_ahead(AHEAD)
            for copy in pattern_arrives():
                copy.wait_recv()
            for copy in pattern_copies():
                copy.wait_send()

        find(level)

        @pl.when(level >= 2)
        def _():
            sent(p_next)

        @pl.when(level == LEV - 1)
        def _():
            give(range(ROWS - CAP))
            for t in range(SENT):
                for copy in direct(t) + [forward(t)]:
                    copy.wait_send()

        @pl.when((level >= 2) & (level <= 4))
        def _():
            pass_on(3 * level - 3)

        @pl.when((level == 5) | (level == 6))
        def _():
            pass_on(2 * level + 2)

        for dx in (0, 1, 3, 2):
            spread_group(p, dx).wait_recv()
            across(p, dx, q).start()

        @pl.when(level == 1)
        def _():
            for t in range(1, EARLY):
                pass_on(t)
            send_ahead(EARLY)
            send_ahead(EARLY + 1)
            for t in range(EARLY):
                arrive(t)
            send_ahead(EARLY + 2)

        @pl.when((level >= 2) & (level <= 4))
        def _():
            for i in (1, 2):
                pass_on(3 * level - 3 + i)
            send_ahead(3 * level)
            for i in range(3):
                arrive(3 * level - 3 + i)
                from_late(3 * level - 3 + i).start()
            send_ahead(3 * level + 1)
            send_ahead(3 * level + 2)

        @pl.when(level == 5)
        def _():
            pass_on(jnp.int32(13))

        @pl.when(level >= 5)
        def _():
            arrive(level + 7)
            from_late(level + 7).start()

        for dx in range(4):
            across(p, dx, 1 - q).wait_recv()

        def to_table(i, carry):
            a, b = i // 4, lax.rem(i, 4)
            for core in range(2):
                for c in range(CAP):
                    table[(((level - 1) * 2 + core) * 16 + i) * CAP + c] = land[p, core, a, b, c]
            return carry

        lax.fori_loop(0, 16, to_table, 0, unroll=4)

        @pl.when((level >= 2) & (level <= 4))
        def _():
            for i in range(3):
                from_late(3 * level - 3 + i).wait()

        @pl.when(level >= 5)
        def _():
            from_late(level + 7).wait()

        for c in range(CAP):
            r = rows[c]
            total = None
            for k in range(0, 4 * SLOTS, 20):
                pieces = [table[lookup[c * 4 * SLOTS + k + i]] for i in range(20)]
                factors = [blocks[places[c], lax.rem(z + (k + i) // SLOTS, 4), (k + i) % SLOTS] for i in range(20)]
                term = dot_t(jnp.concatenate(pieces, axis=1), jnp.concatenate(factors, axis=1))
                total = term if total is None else total + term
            v = times_inverse(rhs[r] - total, inv_terms[r])
            sol[level * CAP + c] = v
            land[p_next, q, x, y, c] = v.astype(jnp.bfloat16)

        for dx in range(4):
            across(p, dx, q).wait_send()

        @pl.when(level < LEV - 1)
        def _():
            start_spread(p_next)

        return carry

    lax.fori_loop(1, LEV, body, 0)
    sent((LEV - 2) % 2)

    give(range(ROWS - CAP, ROWS))


def per_device(factor_blocks, pattern, levels, diag_inverse, right_side):
    bf, f32, dma = jnp.bfloat16, jnp.float32, pltpu.SemaphoreType.DMA
    vmem = pltpu.VMEM
    out = pl.pallas_call(
        kernel,
        out_shape=pltpu.VMEM((ROWS, W, B), f32),
        in_specs=[
            pl.BlockSpec(memory_space=pl.ANY),
            pl.BlockSpec(memory_space=pltpu.SMEM),
            pl.BlockSpec(memory_space=pltpu.SMEM),
            pl.BlockSpec(memory_space=pl.ANY),
            pl.BlockSpec(memory_space=pl.ANY),
        ],
        out_specs=pl.BlockSpec(memory_space=pltpu.VMEM),
        scratch_shapes=[
            vmem((ROWS, SLOTS, B, B), bf),
            vmem((SENT, 4, SLOTS, B, B), bf),
            vmem((SENT - EARLY, 4, SLOTS, B, B), bf),
            vmem((CAP, B, B), f32),
            vmem((ROWS, B, B), f32),
            vmem((ROWS, 2 * B, B), bf),
            vmem((ROWS, W, B), f32),
            pltpu.SMEM((3, SLOTS, ROWS), jnp.int32),
            vmem((EMPTY + 1, W, B), bf),
            vmem((2, 2, 4, 4, CAP, W, B), bf),
            vmem((LEV * CAP, W, B), f32),
            pltpu.SMEM((CAP * 4 * SLOTS,), jnp.int32),
            pltpu.SMEM((CAP,), jnp.int32),
            pltpu.SMEM((CAP,), jnp.int32),
            dma((5,)), dma((SENT - EARLY,)), dma((3,)), dma((3,)),
            dma((SENT, 3)), dma((SENT, 3)),
            dma((2, 4)), dma((2, 4)), dma((2, 4)), dma((2, 4)),
        ],
        compiler_params=pltpu.CompilerParams(
            collective_id=0, has_side_effects=True, vmem_limit_bytes=56 * 1024 * 1024
        ),
    )(factor_blocks, pattern.T, levels, diag_inverse, jnp.swapaxes(right_side, 1, 2))
    return jnp.swapaxes(out, 1, 2)


def solution(mesh):
    return jax.shard_map(
        per_device,
        mesh=mesh,
        in_specs=(
            P("row", "col", None, None),
            P("row", "col"),
            P(),
            P("row", None, None),
            P("row", None, "col"),
        ),
        out_specs=P("row", None, "col"),
        check_vma=False,
    )
```

```python
import jax
import jax.numpy as jnp
from jax import lax
from jax.experimental import pallas as pl
from jax.experimental.pallas import tpu as pltpu
from jax.sharding import PartitionSpec as P

MESH = pl.DeviceIdType.MESH
LEV = 8
CAP = 3
B = 128
W = 32
ROWS = 16
SLOTS = 5
EMPTY = (LEV - 1) * 32 * CAP
SENT = ROWS - 1
EARLY = 3
AHEAD = 2


def dot_t(a, b):
    return lax.dot_general(a, b, (((1,), (1,)), ((), ())), preferred_element_type=jnp.float32)


def split(a):
    high = a.astype(jnp.bfloat16)
    return high, (a - high.astype(jnp.float32)).astype(jnp.bfloat16)


def both_terms(d):
    return jnp.concatenate(split(d), axis=0)


def times_inverse(v, d):
    n = v.shape[0]
    v_high, v_low = split(v)
    terms = dot_t(jnp.concatenate([v_high, v_low], axis=0), d)
    return terms[:n, :B] + (terms[n:, :B] + terms[:n, B:])


def kernel(
    factor, pattern, levels, inverse, right, out,
    raw, blocks, late, inv0, inv, inv_terms, rhs, pats, table, land, sol, lookup, rows, places,
    local_sem, late_sem, pat_s, pat_r, zs, zr, gs, gr, cs, cr,
):
    row, z = lax.axis_index("row"), lax.axis_index("col")
    x, y, q = row // 8, lax.rem(row // 2, 4), lax.rem(row, 2)
    chip = x * 4 + y
    partner = (chip * 2 + 1 - q, z)

    def along_z(by):
        return (row, lax.rem(z + by, 4))

    def remote(src, dst, s, r, to):
        return pltpu.make_async_remote_copy(
            src_ref=src, dst_ref=dst, send_sem=s, recv_sem=r, device_id=to, device_id_type=MESH
        )

    own = [
        pltpu.make_async_copy(inverse.at[0:CAP], inv0, local_sem.at[0]),
        pltpu.make_async_copy(inverse, inv, local_sem.at[1]),
        pltpu.make_async_copy(factor, raw, local_sem.at[2]),
        pltpu.make_async_copy(right.at[0:CAP], rhs.at[0:CAP], local_sem.at[3]),
        pltpu.make_async_copy(right.at[CAP:ROWS], rhs.at[CAP:ROWS], local_sem.at[4]),
    ]

    offsets = [(dx, dy) for dx in range(4) for dy in range(4) if (dx, dy) != (0, 0)]
    offsets.sort(key=lambda o: -(min(o[0], 4 - o[0]) + min(o[1], 4 - o[1])))

    def in_plane(dx, dy):
        return ((lax.rem(x + dx, 4) * 4 + lax.rem(y + dy, 4)) * 2 + q, z)

    barrier = pltpu.get_barrier_semaphore()
    greeted = [partner] + [along_z(by) for by in (1, 2, 3)] + [in_plane(*o) for o in offsets]
    for to in greeted:
        pl.semaphore_signal(barrier, inc=1, device_id=to, device_id_type=MESH)
    for i in (2, 0, 3, 1, 4):
        own[i].start()
    table[EMPTY] = jnp.zeros(table.shape[1:], table.dtype)

    def count_below(level):
        count = jnp.int32(0)
        for r in range(ROWS):
            count += (levels[row * ROWS + r] < level).astype(jnp.int32)
        return count

    skipped = count_below(1)
    own[2].wait()
    for n in range(EARLY):
        blocks[n, z] = raw[jnp.minimum(skipped + n, ROWS - 1)]

    def shift(n, carry):
        late[n - EARLY, z] = raw[jnp.minimum(skipped + n, ROWS - 1)]
        return carry

    lax.fori_loop(EARLY, SENT, shift, 0)
    pl.semaphore_wait(barrier, len(greeted))

    def home(t, owner):
        if isinstance(t, int) and t < EARLY:
            return blocks.at[t, owner]
        return late.at[t - EARLY, owner]

    def direct(t):
        return [remote(home(t, z), home(t, z), zs.at[t, k], zr.at[t, k], along_z(1 + 2 * k)) for k in range(2)]

    def arrives(t, k, owner):
        unit = home(t, owner)
        return remote(unit, unit, zs.at[t, k], zr.at[t, k], along_z(1))

    def forward(t):
        by = 1 + 2 * lax.rem(t + q, 2)
        unit = home(t, lax.rem(z + 4 - by, 4))
        return remote(unit, unit, zs.at[t, 2], zr.at[t, 2], along_z(by))

    def pass_on(t):
        k = lax.rem(t + q, 2)
        arrives(t, k, lax.rem(z + 3 - 2 * k, 4)).wait_recv()
        forward(t).start()

    def send_ahead(t):
        for copy in direct(t):
            copy.start()

    def arrive(t):
        k = lax.rem(t + q, 2)
        arrives(t, 1 - k, lax.rem(z + 1 + 2 * k, 4)).wait_recv()
        arrives(t, 2, lax.rem(z + 2, 4)).wait_recv()

    def pattern_copies():
        return [remote(pattern, pats.at[3 - by], pat_s.at[by - 1], pat_r.at[by - 1], along_z(by)) for by in (1, 2, 3)]

    def pattern_arrives():
        return [remote(pats.at[3 - by], pats.at[3 - by], pat_s.at[by - 1], pat_r.at[by - 1], along_z(by)) for by in (1, 2, 3)]

    for copy in pattern_copies():
        copy.start()
    for t in range(AHEAD):
        send_ahead(t)

    def spread(p, dx, dy):
        unit = land.at[p, q, x, y]
        return remote(unit, unit, gs.at[p, dx], gr.at[p, dx], in_plane(dx, dy))

    def spread_group(p, dx):
        unit = land.at[p, q, lax.rem(x + 4 - dx, 4), pl.ds(0, 4 if dx else 3)]
        return remote(unit, unit, gs.at[p, dx], gr.at[p, dx], partner)

    def across(p, dx, core):
        unit = land.at[p, core, lax.rem(x + 4 - dx, 4)]
        return remote(unit, unit, cs.at[p, dx], cr.at[p, dx], partner)

    def start_spread(p):
        for o in offsets:
            spread(p, *o).start()

    own[0].wait()
    own[3].wait()
    for c in range(CAP):
        v = times_inverse(rhs[c], both_terms(inv0[c]))
        sol[c] = v
        land[0, q, x, y, c] = v.astype(jnp.bfloat16)
    start_spread(0)
    own[1].wait()
    own[4].wait()

    def prepare(r, carry):
        inv_terms[r] = both_terms(inv[r])
        return carry

    lax.fori_loop(0, ROWS, prepare, 0)

    def find(level):
        start = count_below(level)
        for c in range(CAP):
            r = jnp.minimum(start + c, ROWS - 1)
            rows[c] = r
            places[c] = jnp.clip(r - skipped, 0, SENT - 1)
            for k in range(4 * SLOTS):
                far, slot = k // SLOTS, k % SLOTS
                j = pattern[slot, r] if far == 0 else pats[far - 1, slot, r]
                j0 = jnp.maximum(j, 0)
                inside = lax.rem(j0, ROWS)
                its = levels[j0]
                rank = ((levels[jnp.maximum(j0 - 1, 0)] == its) & (inside >= 1)).astype(jnp.int32) + (
                    (levels[jnp.maximum(j0 - 2, 0)] == its) & (inside >= 2)
                ).astype(jnp.int32)
                group = j0 // ROWS
                at = ((its * 2 + lax.rem(group, 2)) * 16 + group // 2) * CAP + rank
                lookup[c * 4 * SLOTS + k] = jnp.where(j < 0, EMPTY, jnp.minimum(at, EMPTY))

    def from_late(t):
        return pltpu.make_async_copy(late.at[t - EARLY], blocks.at[t], late_sem.at[t - EARLY])

    def sent(p):
        for dx in range(4):
            spread_group(p, dx).wait_send()

    def give(some):
        for r in some:
            its = levels[row * ROWS + r]
            rank = jnp.int32(0)
            for back in (1, 2):
                if r >= back:
                    rank += (levels[row * ROWS + r - back] == its).astype(jnp.int32)
            out[r] = sol[its * CAP + rank]

    def body(level, carry):
        p = lax.rem(level - 1, 2)
        p_next = lax.rem(level, 2)

        @pl.when(level == 1)
        def _():
            pass_on(0)
            send_ahead(AHEAD)
            for copy in pattern_arrives():
                copy.wait_recv()
            for copy in pattern_copies():
                copy.wait_send()

        find(level)

        @pl.when(level >= 2)
        def _():
            sent(p_next)

        @pl.when(level == LEV - 1)
        def _():
            give(range(ROWS - CAP))

        @pl.when((level >= 2) & (level <= 4))
        def _():
            pass_on(3 * level - 3)

        @pl.when((level == 5) | (level == 6))
        def _():
            pass_on(2 * level + 2)

        for dx in (1, 3, 0, 2):
            spread_group(p, dx).wait_recv()
            across(p, dx, q).start()

        @pl.when(level == 1)
        def _():
            for t in range(1, EARLY):
                pass_on(t)
            send_ahead(EARLY)
            send_ahead(EARLY + 1)
            for t in range(EARLY):
                arrive(t)
            send_ahead(EARLY + 2)

        @pl.when((level >= 2) & (level <= 4))
        def _():
            for i in (1, 2):
                pass_on(3 * level - 3 + i)
            send_ahead(3 * level)
            for i in range(3):
                arrive(3 * level - 3 + i)
                from_late(3 * level - 3 + i).start()
            send_ahead(3 * level + 1)
            send_ahead(3 * level + 2)

        @pl.when(level == 5)
        def _():
            pass_on(jnp.int32(13))

        @pl.when(level >= 5)
        def _():
            arrive(level + 7)
            from_late(level + 7).start()

        for dx in range(4):
            across(p, dx, 1 - q).wait_recv()

        def to_table(i, carry):
            a, b = i // 4, lax.rem(i, 4)
            for core in range(2):
                for c in range(CAP):
                    table[(((level - 1) * 2 + core) * 16 + i) * CAP + c] = land[p, core, a, b, c]
            return carry

        lax.fori_loop(0, 16, to_table, 0, unroll=4)

        @pl.when((level >= 2) & (level <= 4))
        def _():
            for i in range(3):
                from_late(3 * level - 3 + i).wait()

        @pl.when(level >= 5)
        def _():
            from_late(level + 7).wait()

        for c in range(CAP):
            r = rows[c]
            total = None
            for k in range(0, 4 * SLOTS, 20):
                pieces = [table[lookup[c * 4 * SLOTS + k + i]] for i in range(20)]
                factors = [blocks[places[c], lax.rem(z + (k + i) // SLOTS, 4), (k + i) % SLOTS] for i in range(20)]
                term = dot_t(jnp.concatenate(pieces, axis=1), jnp.concatenate(factors, axis=1))
                total = term if total is None else total + term
            v = times_inverse(rhs[r] - total, inv_terms[r])
            sol[level * CAP + c] = v
            land[p_next, q, x, y, c] = v.astype(jnp.bfloat16)

        for dx in range(4):
            across(p, dx, q).wait_send()

        @pl.when(level < LEV - 1)
        def _():
            start_spread(p_next)

        return carry

    lax.fori_loop(1, LEV, body, 0)
    sent((LEV - 2) % 2)

    for t in range(SENT):
        for copy in direct(t) + [forward(t)]:
            copy.wait_send()
    give(range(ROWS - CAP, ROWS))


def per_device(factor_blocks, pattern, levels, diag_inverse, right_side):
    bf, f32, dma = jnp.bfloat16, jnp.float32, pltpu.SemaphoreType.DMA
    vmem = pltpu.VMEM
    out = pl.pallas_call(
        kernel,
        out_shape=pltpu.VMEM((ROWS, W, B), f32),
        in_specs=[
            pl.BlockSpec(memory_space=pl.ANY),
            pl.BlockSpec(memory_space=pltpu.SMEM),
            pl.BlockSpec(memory_space=pltpu.SMEM),
            pl.BlockSpec(memory_space=pl.ANY),
            pl.BlockSpec(memory_space=pl.ANY),
        ],
        out_specs=pl.BlockSpec(memory_space=pltpu.VMEM),
        scratch_shapes=[
            vmem((ROWS, SLOTS, B, B), bf),
            vmem((SENT, 4, SLOTS, B, B), bf),
            vmem((SENT - EARLY, 4, SLOTS, B, B), bf),
            vmem((CAP, B, B), f32),
            vmem((ROWS, B, B), f32),
            vmem((ROWS, 2 * B, B), bf),
            vmem((ROWS, W, B), f32),
            pltpu.SMEM((3, SLOTS, ROWS), jnp.int32),
            vmem((EMPTY + 1, W, B), bf),
            vmem((2, 2, 4, 4, CAP, W, B), bf),
            vmem((LEV * CAP, W, B), f32),
            pltpu.SMEM((CAP * 4 * SLOTS,), jnp.int32),
            pltpu.SMEM((CAP,), jnp.int32),
            pltpu.SMEM((CAP,), jnp.int32),
            dma((5,)), dma((SENT - EARLY,)), dma((3,)), dma((3,)),
            dma((SENT, 3)), dma((SENT, 3)),
            dma((2, 4)), dma((2, 4)), dma((2, 4)), dma((2, 4)),
        ],
        compiler_params=pltpu.CompilerParams(
            collective_id=0, has_side_effects=True, vmem_limit_bytes=56 * 1024 * 1024
        ),
    )(factor_blocks, pattern.T, levels, diag_inverse, jnp.swapaxes(right_side, 1, 2))
    return jnp.swapaxes(out, 1, 2)


def solution(mesh):
    return jax.shard_map(
        per_device,
        mesh=mesh,
        in_specs=(
            P("row", "col", None, None),
            P("row", "col"),
            P(),
            P("row", None, None),
            P("row", None, "col"),
        ),
        out_specs=P("row", None, "col"),
        check_vma=False,
    )
```
